256 devices in a mesh: tok: 16 (over y_lo, z), voc: 16 (over y_hi, x, core).
Axes of the slice: x: 4, y: 4 (y_hi: 2, y_lo: 2; y = y_hi * 2 + y_lo), z: 8, core: 2. Of those that a mesh axis runs over, the one named last changes fastest.
Arguments:
- hidden: bfloat16 [1024, 8192], P('tok', 'voc'), may hold values from -200 to 200
- gain: float32 [8192], replicated, may hold values from 0.5 to 1.5
- head_weight: bfloat16 [8192, 131072], P(None, ('tok', 'voc')), may hold values from -10 to 10
- student: bfloat16 [1024, 131072], P(None, ('tok', 'voc')), may hold values from -30 to -2
- token_ids: int32 [1024], replicated, may hold values from 0 to 131071
- lengths: int32 [16], replicated, may hold values from 1 to 64
Outputs:
- divergence: float32 [1024], P('tok')
- token_logprob: float32 [1024], P('tok')
The draws below stay inside these ranges and needn't reach their ends.
All inputs are finite; a program needn't handle non-finite values.
Results may differ from the reference program's by a relative error of at most 0.0023.
Values may be sent and summed in bfloat16 or wider, within the bound.
A program may use at most 128 MiB of HBM per device.

```python
import jax
import jax.numpy as jnp
from jax import lax

D = 8192
V = 131072
LEN = 64
TOKENS = 1024
SEQS = 16


def topic_basis(key):
    basis = jnp.clip(jax.random.normal(jax.random.fold_in(key, 51), (D, 16), jnp.float32), -3.0, 3.0)
    order = jax.random.permutation(jax.random.fold_in(key, 52), V)[:64]
    levels = jax.random.uniform(jax.random.fold_in(key, 53), (64,), jnp.float32, 4.0, 16.0)
    return (basis, order, levels)


def draw_hidden(key, part):
    basis, order, levels = topic_basis(key)
    key = jax.random.fold_in(key, 3)
    values = jnp.clip(jax.random.normal(key, (TOKENS, D), jnp.float32), -6.0, 6.0)
    topics = basis.T
    picks = jax.random.randint(jax.random.fold_in(key, 9), (TOKENS, 3), 0, 16)
    weights = jax.random.uniform(jax.random.fold_in(key, 11), (TOKENS, 3), jnp.float32, 0.5, 1.5)
    for index in range(3):
        values = values + weights[:, index:index + 1] * topics[picks[:, index]]
    return values.astype(jnp.bfloat16)


def draw_head_weight(key, part):
    basis, order, levels = topic_basis(key)
    key = jax.random.fold_in(key, 7)
    values = jnp.clip(jax.random.normal(key, (D, V), jnp.float32), -6.0, 6.0) * D ** (-0.5)
    block_count = (V + 511) // 512
    block_of = jnp.arange(V, dtype=jnp.int32) // 512
    block_scale = jnp.exp(jax.random.uniform(jax.random.fold_in(key, 13), (block_count,), jnp.float32, -0.916291, 1.386294))
    column_jitter = jax.random.uniform(jax.random.fold_in(key, 17), (V,), jnp.float32, 0.75, 1.25)
    values = values * (block_scale[block_of] * column_jitter)[None, :]
    topic_of = jnp.arange(64, dtype=jnp.int32) // 4
    boosted = values[:, order] + basis[:, topic_of] * (levels[None, :] / D)
    values = values.at[:, order].set(boosted)
    return values.astype(jnp.bfloat16)


def with_ends(values, stream_key, low, top_value):
    place = [jax.random.randint(jax.random.fold_in(stream_key, axis), (), 0, length) for axis, length in enumerate(values.shape)]
    longest = values.shape.index(max(values.shape))
    beside = place[:longest] + [(place[longest] + 1) % values.shape[longest]] + place[longest + 1:]
    return values.at[tuple(place)].set(low).at[tuple(beside)].set(top_value)


def steps_of(stream_key, extent, pieces, least, high):
    loudness = 1.0
    for axis_at, shards_of in pieces:
        steps = jax.random.uniform(jax.random.fold_in(jax.random.fold_in(stream_key, 6), axis_at), (shards_of,), jnp.float32, least / len(pieces), high / len(pieces))
        loudness = loudness * jnp.repeat(jnp.exp(steps), extent[axis_at] // shards_of).reshape((-1,) + (1,) * (len(extent) - 1 - axis_at))
    return loudness


def setup_inputs(seed: int = 0) -> dict:
    keys = jax.random.split(jax.random.key(seed), 7)
    hidden = draw_hidden(jax.random.fold_in(keys[6], 71), 0)
    gain = jnp.clip(1.0 + 0.1 * jax.random.normal(keys[1], (D,), jnp.float32), 0.5, 1.5)
    head_weight = draw_head_weight(jax.random.fold_in(keys[6], 71), 0)
    student = jnp.clip(-30.0 + 28.0 * jax.random.uniform(keys[3], (TOKENS, V), jnp.float32) ** steps_of(keys[3], (TOKENS, V), ((1, 256),), -0.2, 0.2), -30.0, -2.0).astype(jnp.bfloat16)
    token_ids = with_ends(jax.random.randint(keys[4], (TOKENS,), 0, V), jax.random.fold_in(keys[4], 1), 0, V - 1).astype(jnp.int32)
    lengths = with_ends(jax.random.randint(keys[5], (SEQS,), 1, LEN + 1), jax.random.fold_in(keys[5], 1), 1, LEN).astype(jnp.int32)
    return {"hidden": hidden, "gain": gain, "head_weight": head_weight, "student": student, "token_ids": token_ids, "lengths": lengths}


EPS = 1e-06

def reference(hidden, gain, head_weight, student, token_ids, lengths):
    hf = hidden.astype(jnp.float32)
    squares = lax.optimization_barrier(jnp.sum(hf * hf, axis=1))
    normed = (hf * lax.rsqrt(squares / D + EPS)[:, None] * gain[None, :]).astype(jnp.bfloat16)
    logits = jnp.dot(normed, head_weight, preferred_element_type=jnp.float32)
    top = lax.optimization_barrier(jnp.max(logits, axis=1))
    total = lax.optimization_barrier(jnp.sum(jnp.exp(logits - top[:, None]), axis=1))
    lse = top + jnp.log(total)
    shifted = logits - lse[:, None]
    kl = lax.optimization_barrier(jnp.sum(jnp.exp(shifted) * (shifted - student.astype(jnp.float32)), axis=1))
    picked = jnp.take_along_axis(logits, token_ids.astype(jnp.int32)[:, None], axis=1)[:, 0] - lse
    positions = jnp.arange(TOKENS, dtype=jnp.int32)
    valid = positions % LEN < lengths[positions // LEN]
    divergence = jnp.where(valid, kl, jnp.float32(0.0))
    token_logprob = jnp.where(valid, picked, jnp.float32(0.0))
    return (divergence, token_logprob)
```

```python
import functools

import jax
import jax.numpy as jnp
from jax import lax
from jax.experimental import pallas as pl
from jax.experimental.pallas import tpu as pltpu
from jax.sharding import PartitionSpec as P

D = 8192
LEN = 64
EPS = 1e-06
MESH = pl.DeviceIdType.MESH
F32 = jnp.float32
BF16 = jnp.bfloat16
RING = {"y": 4, "x": 4, "z": 8}
NMSG = 40
VALL = slice(None)


def split3(value):
    hi = value.astype(BF16).astype(F32)
    rest = value - hi
    mid = rest.astype(BF16).astype(F32)
    return hi, mid, (rest - mid).astype(BF16).astype(F32)


def kernel(parts, cap, hidden, gain, lens, ids, student, head, out, *scratch):
    slabs = scratch[: len(parts)]
    (w_all, st_all, onehot, st_rows, id_cols, acc, stats, scaled, sq_buf, a2a_out, a2a_in,
     fin_out, fin_a, fin_b, local_sem, pair_sem, send_sem, recv_sem) = scratch[len(parts):]
    tok = lax.axis_index("tok")
    voc = lax.axis_index("voc")
    here = {"y": (voc // 8) * 2 + tok // 8, "x": (voc // 2) % 4, "z": tok % 8}
    core = voc % 2

    def device(place, which):
        return {"tok": (place["y"] % 2) * 8 + place["z"], "voc": ((place["y"] // 2) * 4 + place["x"]) * 2 + which}

    def moved(axis, by):
        place = dict(here)
        place[axis] = lax.rem(here[axis] + by + RING[axis], RING[axis])
        return place

    def tok_peer(step):
        return {"tok": lax.rem(tok + step, 16), "voc": voc}

    def voc_peer(step):
        return {"tok": tok, "voc": lax.rem(voc + step, 16)}

    barrier = pltpu.get_barrier_semaphore()

    def greet(step, carry):
        pl.semaphore_signal(barrier, inc=1, device_id=tok_peer(step), device_id_type=MESH)
        pl.semaphore_signal(barrier, inc=1, device_id=voc_peer(step), device_id_type=MESH)
        return carry

    lax.fori_loop(1, 16, greet, 0)
    across = {"tok": lax.rem(tok + 8, 16), "voc": lax.rem(voc + 8, 16)}
    pl.semaphore_signal(barrier, inc=1, device_id=across, device_id_type=MESH)

    def head_copy(index):
        y = (index // 16) * 2 + index % 2
        return pltpu.make_async_copy(
            head.at[index], w_all.at[(index // 2) % 2, y, (index // 4) % 4], local_sem.at[index]
        )

    student_copy = pltpu.make_async_copy(student, st_all, local_sem.at[32])
    student_copy.start()

    def load(index, carry):
        head_copy(index).start()
        return carry

    lax.fori_loop(0, 32, load, 0)

    rows = hidden[...].astype(F32)
    rows = jnp.concatenate([rows, rows], axis=0)
    turned = rows.T
    square = jnp.sum(turned * turned, axis=0, keepdims=True)
    sq_buf[0] = jnp.broadcast_to(square, (8, 128))
    gain_dev = gain[:, pl.ds(pl.multiple_of(voc * 512, 512), 512)]
    scaled[...] = (rows * gain_dev).T

    pl.semaphore_wait(barrier, 31)

    def sq_copy(step):
        return pltpu.make_async_remote_copy(
            src_ref=sq_buf.at[0], dst_ref=sq_buf.at[step], send_sem=pair_sem.at[0, step],
            recv_sem=pair_sem.at[1, step], device_id=voc_peer(step), device_id_type=MESH)

    def a2a_copy(step):
        return pltpu.make_async_remote_copy(
            src_ref=a2a_out.at[lax.rem(tok + step, 16)], dst_ref=a2a_in.at[tok], send_sem=pair_sem.at[2, step],
            recv_sem=pair_sem.at[3, step], device_id=tok_peer(step), device_id_type=MESH)

    def fin_a_copy(step):
        return pltpu.make_async_remote_copy(
            src_ref=fin_out.at[lax.rem(tok + step, 16) // 2], dst_ref=fin_a.at[step], send_sem=pair_sem.at[4, step],
            recv_sem=pair_sem.at[5, step], device_id=tok_peer(step), device_id_type=MESH)

    def fin_b_copy(step):
        return pltpu.make_async_remote_copy(
            src_ref=fin_b.at[0], dst_ref=fin_b.at[step], send_sem=pair_sem.at[6, step],
            recv_sem=pair_sem.at[7, step], device_id=voc_peer(step), device_id_type=MESH)

    def start_all(copy):
        def body(step, carry):
            copy(step).start()
            return carry
        lax.fori_loop(1, 16, body, 0)

    def recv_all(copy):
        def body(step, carry):
            copy(step).wait_recv()
            return carry
        lax.fori_loop(1, 16, body, 0)

    def sent_all(copy):
        def body(step, carry):
            copy(step).wait_send()
            return carry
        lax.fori_loop(1, 16, body, 0)

    start_all(sq_copy)

    lane = lax.broadcasted_iota(jnp.int32, (1, 128), 1)
    place_of = []
    offset = jnp.int32(0)
    for pair in range(8):
        first, second = lens[2 * pair], lens[2 * pair + 1]
        low = jnp.where(lane < first, offset + lane, -1)
        high = jnp.where(lane - 64 < second, offset + first + lane - 64, -1)
        place_of.append(jnp.where(lane < 64, low, high))
        offset = offset + first + second
    place_of = jnp.concatenate(place_of, axis=1)

    def fill(block, carry):
        start = pl.multiple_of(block * 64, 64)
        want = lax.broadcasted_iota(jnp.int32, (64, 1024), 0) + start
        onehot[pl.ds(start, 64), :] = jnp.where(want == place_of, 1.0, 0.0).astype(BF16)
        return carry

    lax.fori_loop(0, cap // 64, fill, 0)

    recv_all(sq_copy)
    total_sq = sq_buf[0]
    for step in range(1, 16):
        total_sq = total_sq + sq_buf[step]
    inv = lax.rsqrt(total_sq / D + EPS)
    normed = (scaled[...].reshape(64, 8, 128) * inv[None]).reshape(16, 32, 128).astype(BF16)
    a2a_out[...] = normed
    start_all(a2a_copy)
    a2a_in[tok] = a2a_out[tok]

    local_id = ids[...] - (tok * 16 + voc) * 512
    local_id = jnp.where((local_id >= 0) & (local_id < 512), local_id, 512)
    digits = jnp.where(lax.broadcasted_iota(jnp.int32, (16, 1024), 0) == 0, local_id // 256, local_id % 256)
    digits = digits.astype(F32).astype(BF16)
    cols = lax.dot_general(onehot[...], digits, (((1,), (1,)), ((), ())), preferred_element_type=F32)
    id_cols[...] = cols[:, 0:1] * 256.0 + cols[:, 1:2]

    recv_all(a2a_copy)
    pieces = [jnp.where(lane < 64, a2a_in[2 * pair], a2a_in[2 * pair + 1]) for pair in range(8)]
    block = jnp.concatenate(pieces, axis=1)
    packed = lax.dot_general(block, onehot[...], (((1,), (1,)), ((), ())), preferred_element_type=F32).astype(BF16)

    sends = []

    def push(number, index, src, target):
        copy = pltpu.make_async_remote_copy(
            src_ref=src, dst_ref=src, send_sem=send_sem.at[number, index], recv_sem=recv_sem.at[number, index],
            device_id=target, device_id_type=MESH)
        copy.start()
        sends.append(copy)
        return copy

    def view(number, which, y=None, x=None, z=None):
        ref = slabs[number]
        pick = [VALL if at is None else at for at in (y, x, z)]
        return ref.at[(which, *pick)]

    def plane(number, which, at, half=None):
        last = parts[number][4]
        if last == "z":
            return view(number, which, y=None if half is None else pl.ds(2 * half, 2), z=at)
        if last == "x":
            return view(number, which, y=None if half is None else pl.ds(2 * half, 2), x=at)
        return view(number, which, y=at, x=None if half is None else pl.ds(2 * half, 2))

    count = range(len(parts))
    y, x, z = here["y"], here["x"], here["z"]
    stage1 = []
    for n in count:
        lane0, wide, row0, deep, last = parts[n]
        slabs[n][core, y, x, z] = packed[row0:row0 + deep, lane0:lane0 + wide]
        first = "x" if last == "z" else "z"
        own = slabs[n].at[core, y, x, z]
        stage1.append([push(n, by, own, device(moved(first, by), core)) for by in range(1, RING[first])])

    def line(n, at, half=None):
        last = parts[n][4]
        if last == "z":
            return view(n, core, y=at, x=None if half is None else pl.ds(2 * half, 2), z=z)
        if last == "x":
            return view(n, core, y=at, x=x, z=None if half is None else pl.ds(4 * half, 4))
        return view(n, core, y=y, x=at, z=None if half is None else pl.ds(4 * half, 4))

    second = ["x" if part[4] == "y" else "y" for part in parts]
    stage2 = []
    for n in count:
        for copy in stage1[n]:
            copy.wait_recv()
        axis = second[n]
        own = line(n, here[axis])
        stage2.append([push(n, 8, own, device(moved(axis, 1), core)), push(n, 9, own, device(moved(axis, -1), core))])
    for n in count:
        axis = second[n]
        stage2[n][0].wait_recv()
        far = [push(n, 10, line(n, moved(axis, -1)[axis], 0), device(moved(axis, 1), core))]
        stage2[n][1].wait_recv()
        far.append(push(n, 11, line(n, moved(axis, 1)[axis], 1), device(moved(axis, -1), core)))
        stage2[n] = far

    mate = device(here, 1 - core)
    sibs = [[] for _ in count]
    flight = {}
    for n in count:
        for copy in stage2[n]:
            copy.wait_recv()
        axis = parts[n][4]
        for half in (0, 1):
            flight[n, 1, 0, half] = push(n, 12 + half, plane(n, core, here[axis], half), device(moved(axis, 1), core))
            flight[n, -1, 0, 1 - half] = push(
                n, 20 + half, plane(n, core, here[axis], 1 - half), device(moved(axis, -1), core))
        sibs[n].append((0, push(n, 28, plane(n, core, here[axis]), mate)))

    def multiply(n, which, by, fresh=False):
        lane0, wide, row0, deep, last = parts[n]
        at = moved(last, by)[last]
        pick = tuple(at if axis == last else VALL for axis in ("y", "x", "z"))
        deep_all = 128 // RING[last] * deep
        left = slabs[n][(which, *pick)].reshape(deep_all, wide)
        right = w_all[(which, *pick, slice(row0, row0 + deep))].reshape(deep_all, 512)
        term = lax.dot_general(left, right, (((0,), (0,)), ((), ())), preferred_element_type=F32)
        if fresh:
            acc[lane0:lane0 + wide, :] = term
        else:
            acc[lane0:lane0 + wide, :] += term

    student_copy.wait()
    st_rows[...] = jnp.dot(onehot[...], st_all[...], preferred_element_type=F32).astype(BF16)

    def loaded(index, carry):
        head_copy(index).wait()
        return carry

    lax.fori_loop(0, 32, loaded, 0)
    started = set()
    todo = []

    def due(n, which, by):
        todo.append((n, which, by))

    def work():
        while todo:
            n, which, by = todo.pop(0)
            lanes = parts[n][0]
            multiply(n, which, by, fresh=lanes not in started)
            started.add(lanes)

    for n in count:
        due(n, core, 0)
    steps = max(RING[part[4]] // 2 for part in parts)
    done_sib = [0] * len(parts)

    def drain_sibs():
        for n in count:
            while done_sib[n] < len(sibs[n]):
                by, copy = sibs[n][done_sib[n]]
                copy.wait_recv()
                due(n, 1 - core, by)
                done_sib[n] += 1

    for step in range(steps):
        late = []
        for n in count:
            axis = parts[n][4]
            last_step = RING[axis] // 2 - 1
            if step > last_step:
                continue
            order = [(1, 0), (-1, 1)] if step == last_step else [(1, 0), (-1, 1), (1, 1), (-1, 0)]
            for way, half in order:
                flight[n, way, step, half].wait_recv()
                at = moved(axis, -way * (step + 1))[axis]
                go_on = step + 1 < last_step or (step + 1 == last_step and (way, half) in ((1, 0), (-1, 1)))
                if go_on:
                    base = 12 if way == 1 else 20
                    slot = 2 * (step + 1) + (half if way == 1 else 1 - half)
                    flight[n, way, step + 1, half] = push(
                        n, base + slot, plane(n, core, at, half), device(moved(axis, way), core))
            if step == last_step:
                by = step + 1
                late.append((n, by, push(n, 29 + 2 * step, plane(n, core, moved(axis, by)[axis]), mate)))
            else:
                for way in (1, -1):
                    by = -way * (step + 1)
                    late.append((n, by, push(
                        n, 29 + 2 * step + (way == 1), plane(n, core, moved(axis, by)[axis]), mate)))
        drain_sibs()
        work()
        for n, by, copy in late:
            sibs[n].append((by, copy))
            due(n, core, by)
    work()
    drain_sibs()
    work()

    lanes128 = lax.broadcasted_iota(jnp.int32, (64, 128), 1)
    lanes512 = lax.broadcasted_iota(jnp.int32, (64, 512), 1).astype(F32)

    def partials(block, carry):
        take = pl.ds(pl.multiple_of(block * 64, 64), 64)
        logits = acc[take, :]
        top = jnp.max(logits, axis=1, keepdims=True)
        low = logits - top
        expo = jnp.exp(low)
        total = jnp.sum(expo, axis=1, keepdims=True)
        cross = jnp.sum(expo * (low - st_rows[take, :].astype(F32)), axis=1, keepdims=True)
        pick = jnp.sum(jnp.where(lanes512 == id_cols[take, :], logits, 0.0), axis=1, keepdims=True)
        table = jnp.zeros((64, 128), F32)
        for at, value in enumerate((top, total, cross, pick)):
            for digit, piece in enumerate(split3(value)):
                table = jnp.where(lanes128 == 8 * digit + at, piece, table)
        stats[take, :] = table.astype(BF16)
        return carry

    lax.fori_loop(0, cap // 64, partials, 0)
    spread = lax.dot_general(stats[...], onehot[...], (((0,), (0,)), ((), ())), preferred_element_type=F32)
    spread = spread[0:8] + spread[8:16] + spread[16:24]
    for pair in range(8):
        fin_out[pair] = spread[:, 128 * pair:128 * (pair + 1)]
    start_all(fin_a_copy)
    fin_a[0] = fin_out[tok // 2]
    recv_all(fin_a_copy)

    def combine(ref):
        every = ref[...]
        top, total, cross, pick = (every[:, k:k + 1, :] for k in range(4))
        most = jnp.max(top, axis=0, keepdims=True)
        gap = top - most
        scale = jnp.exp(gap)
        return (most[0], jnp.sum(scale * total, axis=0), jnp.sum(scale * (cross + gap * total), axis=0),
                jnp.sum(pick, axis=0))

    sub = lax.broadcasted_iota(jnp.int32, (8, 128), 0)

    def table_of(values):
        table = jnp.zeros((8, 128), F32)
        for at, value in enumerate(values):
            table = jnp.where(sub == at, value, table)
        return table

    fin_b[0] = table_of(combine(fin_a))
    start_all(fin_b_copy)
    recv_all(fin_b_copy)
    top, total, cross, pick = combine(fin_b)
    log_total = jnp.log(total)
    kl = cross / total - log_total
    logprob = pick - (top + log_total)
    inside = jnp.where(lane < 64, lane, lane - 64)
    valid = inside < lens[tok]
    result = table_of((jnp.where(valid, kl, 0.0), jnp.where(valid, logprob, 0.0)))
    out[...] = jnp.where(tok % 2 == 0, result, pltpu.roll(result, 64, 1))

    for copy in sends:
        copy.wait_send()
    for copy in (sq_copy, a2a_copy, fin_a_copy, fin_b_copy):
        sent_all(copy)


def parts_of(cap):
    if cap == 512:
        return [(0, 128, 0, 32, "x"), (128, 128, 0, 16, "x"), (256, 128, 0, 32, "y"), (128, 128, 16, 16, "y"),
                (384, 128, 0, 32, "z")]
    if cap == 640:
        return [(0, 256, 0, 32, "x"), (256, 256, 0, 32, "y"), (512, 128, 0, 32, "z")]
    return [(0, 384, 0, 32, "x"), (384, 384, 0, 32, "y"), (768, 256, 0, 32, "z")]


def run(cap, number, hidden, gain, lengths, ids, student, head):
    parts = parts_of(cap)
    vmem = pl.BlockSpec(memory_space=pltpu.VMEM)
    hbm = pl.BlockSpec(memory_space=pl.ANY)
    return pl.pallas_call(
        functools.partial(kernel, parts, cap),
        out_shape=jax.ShapeDtypeStruct((8, 128), F32),
        in_specs=[vmem, vmem, pl.BlockSpec(memory_space=pltpu.SMEM), vmem, hbm, hbm],
        out_specs=vmem,
        scratch_shapes=[pltpu.VMEM((2, 4, 4, 8, part[3], part[1]), BF16) for part in parts] + [
            pltpu.VMEM((2, 4, 4, 8, 32, 512), BF16),
            pltpu.VMEM((1024, 512), BF16),
            pltpu.VMEM((cap, 1024), BF16),
            pltpu.VMEM((cap, 512), BF16),
            pltpu.VMEM((cap, 1), F32),
            pltpu.VMEM((cap, 512), F32),
            pltpu.VMEM((cap, 128), BF16),
            pltpu.VMEM((512, 128), F32),
            pltpu.VMEM((16, 8, 128), F32),
            pltpu.VMEM((16, 32, 128), BF16),
            pltpu.VMEM((16, 32, 128), BF16),
            pltpu.VMEM((8, 8, 128), F32),
            pltpu.VMEM((16, 8, 128), F32),
            pltpu.VMEM((16, 8, 128), F32),
            pltpu.SemaphoreType.DMA((33,)),
            pltpu.SemaphoreType.DMA((8, 16)),
            pltpu.SemaphoreType.DMA((len(parts), NMSG)),
            pltpu.SemaphoreType.DMA((len(parts), NMSG)),
        ],
        compiler_params=pltpu.CompilerParams(
            collective_id=number, has_side_effects=True, vmem_limit_bytes=60 * 1024 * 1024),
        name="gathered_head_%d" % cap,
    )(hidden, gain, lengths, ids, student, head)


CAPS = (1024,)


def per_device(hidden, gain, head_weight, student, token_ids, lengths):
    args = (hidden, gain.reshape(1, D), lengths, token_ids.reshape(1, -1), student,
            head_weight.reshape(32, 8, 32, head_weight.shape[1]))
    if len(CAPS) == 1:
        table = run(CAPS[0], 0, *args)
    else:
        tokens = jnp.sum(lengths)
        which = sum((tokens > cap).astype(jnp.int32) for cap in CAPS[:-1])
        table = lax.switch(which, [functools.partial(run, cap, at) for at, cap in enumerate(CAPS)], *args)
    return table[0, :64], table[1, :64]


def solution(mesh):
    placed = (P("tok", "voc"), P(), P(None, ("tok", "voc")), P(None, ("tok", "voc")), P(), P())
    return jax.shard_map(
        per_device, mesh=mesh, in_specs=placed, out_specs=(P("tok"), P("tok")), check_vma=False
    )
```

```python
import functools

import jax
import jax.numpy as jnp
from jax import lax
from jax.experimental import pallas as pl
from jax.experimental.pallas import tpu as pltpu
from jax.sharding import PartitionSpec as P

D = 8192
LEN = 64
EPS = 1e-06
MESH = pl.DeviceIdType.MESH
F32 = jnp.float32
BF16 = jnp.bfloat16
RING = {"y": 4, "x": 4, "z": 8}
NMSG = 48
VALL = slice(None)


def split3(value):
    hi = value.astype(BF16).astype(F32)
    rest = value - hi
    mid = rest.astype(BF16).astype(F32)
    return hi, mid, (rest - mid).astype(BF16).astype(F32)


def blocks_of(groups):
    blocks = [[] for _ in groups]
    start = 0
    for part, count in enumerate(groups):
        for _ in range(count // 2):
            blocks[part].append((start, 128))
            start += 128
    for part, count in enumerate(groups):
        if count % 2:
            blocks[part].append((start, 64))
            start += 64
    return blocks


def kernel(groups, hidden, gain, lens, ids, student, head, out, *scratch):
    cap = 64 * sum(groups)
    blocks = blocks_of(groups)
    lasts = ("x", "y", "z")
    slabs = scratch[:3]
    (w_all, st_all, h_in, gain_in, ids_in, onehot, st_rows, id_cols, acc, stats, gcol, r_rows, sq_buf, r_buf, a2a_out,
     a2a_in, fin_out, fin_a, fin_b, local_sem, pair_sem, send_sem, recv_sem) = scratch[3:]
    tok = lax.axis_index("tok")
    voc = lax.axis_index("voc")
    here = {"y": (voc // 8) * 2 + tok // 8, "x": (voc // 2) % 4, "z": tok % 8}
    core = voc % 2
    way = 1 - 2 * core

    def device(place, which):
        return {"tok": (place["y"] % 2) * 8 + place["z"], "voc": ((place["y"] // 2) * 4 + place["x"]) * 2 + which}

    def moved(axis, by):
        place = dict(here)
        place[axis] = lax.rem(here[axis] + by + RING[axis], RING[axis])
        return place

    def tok_peer(step):
        return {"tok": lax.rem(tok + step, 16), "voc": voc}

    def voc_peer(step):
        return {"tok": tok, "voc": lax.rem(voc + step, 16)}

    def plane_peer(step):
        return device({"y": lax.rem(here["y"] + step // 4, 4), "x": lax.rem(here["x"] + step % 4, 4), "z": here["z"]}, core)

    barrier = pltpu.get_barrier_semaphore()

    def greet(step, carry):
        pl.semaphore_signal(barrier, inc=1, device_id=tok_peer(step), device_id_type=MESH)
        pl.semaphore_signal(barrier, inc=1, device_id=voc_peer(step), device_id_type=MESH)
        return carry

    lax.fori_loop(1, 16, greet, 0)
    for step in range(4, 16):
        dy, dx = step // 4, step % 4
        if dy % 2 and dx:
            pl.semaphore_signal(barrier, inc=1, device_id=plane_peer(step), device_id_type=MESH)
    across = {"tok": lax.rem(tok + 8, 16), "voc": lax.rem(voc + 8, 16)}
    pl.semaphore_signal(barrier, inc=1, device_id=across, device_id_type=MESH)

    def head_copy(index):
        y = (index // 16) * 2 + index % 2
        return pltpu.make_async_copy(
            head.at[index], w_all.at[(index // 2) % 2, y, (index // 4) % 4], local_sem.at[index]
        )

    hidden_copy = pltpu.make_async_copy(hidden, h_in, local_sem.at[32])
    gain_copy = pltpu.make_async_copy(gain, gain_in, local_sem.at[33])
    ids_copy = pltpu.make_async_copy(ids, ids_in, local_sem.at[34])
    student_copy = pltpu.make_async_copy(student, st_all, local_sem.at[35])
    hidden_copy.start()
    gain_copy.start()
    ids_copy.start()
    student_copy.start()

    def load(index, carry):
        head_copy(index).start()
        return carry

    lax.fori_loop(0, 32, load, 0)

    lane = lax.broadcasted_iota(jnp.int32, (1, 128), 1)
    place_of = []
    offset = jnp.int32(0)
    for pair in range(8):
        first, second = lens[2 * pair], lens[2 * pair + 1]
        low = jnp.where(lane < first, offset + lane, -1)
        high = jnp.where(lane - 64 < second, offset + first + lane - 64, -1)
        place_of.append(jnp.where(lane < 64, low, high))
        offset = offset + first + second
    place_of = jnp.concatenate(place_of, axis=1)

    def fill(block, carry):
        start = pl.multiple_of(block * 64, 64)
        want = lax.broadcasted_iota(jnp.int32, (64, 1024), 0) + start
        onehot[pl.ds(start, 64), :] = jnp.where(want == place_of, 1.0, 0.0).astype(BF16)
        return carry

    lax.fori_loop(0, cap // 64, fill, 0)

    hidden_copy.wait()
    rows = h_in[...].astype(F32)
    rows = jnp.concatenate([rows, rows], axis=0)
    turned = rows.T
    square = jnp.sum(turned * turned, axis=0, keepdims=True)
    sq_buf[0] = jnp.broadcast_to(square, (8, 128))
    a2a_out[...] = turned.reshape(16, 32, 128).astype(BF16)

    gain_copy.wait()

    def spread_gain(row, carry):
        wide = jnp.broadcast_to(gain_in[pl.ds(row, 1), :], (128, 128)).T
        index = row // 2
        y = (index // 16) * 2 + index % 2
        start = pl.multiple_of((row % 2) * 4, 4)
        gcol[(index // 2) % 2, y, (index // 4) % 4, pl.ds(start, 4)] = wide.reshape(4, 32, 128)
        return carry

    lax.fori_loop(0, 64, spread_gain, 0)

    def zero(block, carry):
        acc[pl.ds(pl.multiple_of(block * 64, 64), 64), :] = jnp.zeros((64, 512), F32)
        return carry

    lax.fori_loop(0, cap // 64, zero, 0)

    pl.semaphore_wait(barrier, 37)

    def sq_copy(step):
        return pltpu.make_async_remote_copy(
            src_ref=sq_buf.at[0], dst_ref=sq_buf.at[step], send_sem=pair_sem.at[0, step],
            recv_sem=pair_sem.at[1, step], device_id=voc_peer(step), device_id_type=MESH)

    def a2a_copy(step):
        return pltpu.make_async_remote_copy(
            src_ref=a2a_out.at[lax.rem(tok + step, 16)], dst_ref=a2a_in.at[tok], send_sem=pair_sem.at[2, step],
            recv_sem=pair_sem.at[3, step], device_id=tok_peer(step), device_id_type=MESH)

    def r_copy(step):
        return pltpu.make_async_remote_copy(
            src_ref=r_buf.at[tok], dst_ref=r_buf.at[tok], send_sem=pair_sem.at[8, step],
            recv_sem=pair_sem.at[9, step], device_id=tok_peer(step), device_id_type=MESH)

    def fin_a_copy(step):
        return pltpu.make_async_remote_copy(
            src_ref=fin_out.at[lax.rem(tok + step, 16) // 2], dst_ref=fin_a.at[step], send_sem=pair_sem.at[4, step],
            recv_sem=pair_sem.at[5, step], device_id=tok_peer(step), device_id_type=MESH)

    def fin_b_copy(step):
        return pltpu.make_async_remote_copy(
            src_ref=fin_b.at[0], dst_ref=fin_b.at[step], send_sem=pair_sem.at[6, step],
            recv_sem=pair_sem.at[7, step], device_id=voc_peer(step), device_id_type=MESH)

    def start_all(copy):
        def body(step, carry):
            copy(step).start()
            return carry
        lax.fori_loop(1, 16, body, 0)

    def recv_all(copy):
        def body(step, carry):
            copy(step).wait_recv()
            return carry
        lax.fori_loop(1, 16, body, 0)

    def sent_all(copy):
        def body(step, carry):
            copy(step).wait_send()
            return carry
        lax.fori_loop(1, 16, body, 0)

    start_all(a2a_copy)
    start_all(sq_copy)
    a2a_in[tok] = a2a_out[tok]

    ids_copy.wait()
    local_id = ids_in[...] - (tok * 16 + voc) * 512
    local_id = jnp.where((local_id >= 0) & (local_id < 512), local_id, 512)
    digits = jnp.where(lax.broadcasted_iota(jnp.int32, (16, 1024), 0) == 0, local_id // 256, local_id % 256)
    digits = digits.astype(F32).astype(BF16)
    cols = lax.dot_general(onehot[...], digits, (((1,), (1,)), ((), ())), preferred_element_type=F32)
    id_cols[...] = cols[:, 0:1] * 256.0 + cols[:, 1:2]
    student_copy.wait()
    st_rows[...] = jnp.dot(onehot[...], st_all[...], preferred_element_type=F32).astype(BF16)

    recv_all(a2a_copy)
    pieces = [jnp.where(lane < 64, a2a_in[2 * pair], a2a_in[2 * pair + 1]) for pair in range(8)]
    block = jnp.concatenate(pieces, axis=1)
    packed = lax.dot_general(block, onehot[...], (((1,), (1,)), ((), ())), preferred_element_type=F32)

    sends = []

    def push(number, index, src, target):
        copy = pltpu.make_async_remote_copy(
            src_ref=src, dst_ref=src, send_sem=send_sem.at[number, index], recv_sem=recv_sem.at[number, index],
            device_id=target, device_id_type=MESH)
        copy.start()
        sends.append(copy)
        return copy

    y, x, z = here["y"], here["x"], here["z"]
    own = [slab.at[core, y, x, z] for slab in slabs]
    stage1 = [[], [], []]
    for n in range(3):
        for at, (start, wide) in enumerate(blocks[n]):
            if wide == 128:
                slabs[n][core, y, x, z, 32 * at:32 * at + 32] = packed[:, start:start + 128].astype(BF16)
            else:
                base = start // 128 * 128
                both = packed[:, base:base + 128]
                flipped = pltpu.roll(both, 64, 1)
                if start == base:
                    half = jnp.where(lane < 64, both[0:16], flipped[16:32])
                else:
                    half = jnp.where(lane < 64, flipped[0:16], both[16:32])
                slabs[n][core, y, x, z, 32 * at:32 * at + 16] = half.astype(BF16)
        if n < 2:
            for by in (4, 3, 5, 2, 6, 1, 7):
                stage1[n].append(push(n, by, own[n], device(moved("z", by), core)))
        else:
            for step in (10, 2, 8, 6, 9, 11, 14, 1, 3, 4, 12, 5, 7, 13, 15):
                stage1[n].append(push(n, step, own[n], plane_peer(step)))

    mate = device(here, 1 - core)

    recv_all(sq_copy)
    total_sq = sq_buf[0]
    for step in range(1, 16):
        total_sq = total_sq + sq_buf[step]
    r_buf[tok] = lax.rsqrt(total_sq / D + EPS)
    start_all(r_copy)

    def piece(n, which, c_at, b_at):
        if n == 0:
            return slabs[0].at[which, b_at, c_at]
        return slabs[1].at[which, c_at, b_at]

    def plane(n, which, c_at):
        if n == 0:
            return slabs[0].at[which, :, c_at]
        if n == 1:
            return slabs[1].at[which, c_at]
        return slabs[2].at[which, :, :, c_at]

    def zhalf(c_at, half):
        return slabs[2].at[core, pl.ds(2 * half, 2), :, c_at]

    second = ("y", "x")
    flight = {}

    def both_ways(n, name, b_at, index):
        axis = lasts[n]
        for side in (1, -1):
            flight[n, name, side] = push(
                n, index + (side == 1), piece(n, core, here[axis], b_at), device(moved(axis, side), core))

    def go_on(n, name, b_at, index):
        axis = lasts[n]
        flight[n, name, 1].wait_recv()
        flight[n, name, -1].wait_recv()
        flight[n, name, 2] = push(
            n, index, piece(n, core, moved(axis, -way)[axis], b_at), device(moved(axis, way), core))

    def multiply(n, which, pick):
        for at, (start, wide) in enumerate(blocks[n]):
            if wide == 128:
                left = slabs[n][(which, *pick, slice(32 * at, 32 * at + 32))].reshape(-1, 128)
                depth = left.shape[0]
                factor = r_rows[0:1, start:start + 128]
                weight = gcol[(which, *pick)].reshape(depth, 128)
                left = (left.astype(F32) * factor * weight).astype(BF16)
                right = w_all[(which, *pick)].reshape(depth, 512)
                acc[start:start + 128, :] += lax.dot_general(
                    left, right, (((0,), (0,)), ((), ())), preferred_element_type=F32)
            else:
                left = slabs[n][(which, *pick, slice(32 * at, 32 * at + 16))].reshape(-1, 128)
                depth = left.shape[0]
                base = start // 128 * 128
                factor = r_rows[0:1, base:base + 128]
                flipped = pltpu.roll(factor, 64, 1)
                factor = jnp.where((lane < 64) == (start == base), factor, flipped)
                weight = jnp.where(
                    lane < 64, gcol[(which, *pick, slice(0, 16))].reshape(depth, 128),
                    gcol[(which, *pick, slice(16, 32))].reshape(depth, 128))
                left = (left.astype(F32) * factor * weight).astype(BF16)
                first = w_all[(which, *pick, slice(0, 16))].reshape(depth, 512)
                other = w_all[(which, *pick, slice(16, 32))].reshape(depth, 512)
                top = lax.dot_general(left, first, (((0,), (0,)), ((), ())), preferred_element_type=F32)
                low = lax.dot_general(left, other, (((0,), (0,)), ((), ())), preferred_element_type=F32)
                acc[start:start + 64, :] += top[0:64] + low[64:128]

    def pick_plane(n, by):
        axis = lasts[n]
        at = moved(axis, by)[axis]
        return tuple(at if axis == name else VALL for name in ("y", "x", "z"))

    def pick_piece(n, by, b_at):
        axis = lasts[n]
        at = moved(axis, by)[axis]
        return (b_at, at, VALL) if n == 0 else (at, b_at, VALL)

    todo = []

    def work(limit=99):
        while todo and limit:
            multiply(*todo.pop(0))
            limit -= 1

    waiting = []

    def to_mate(n, index, ref, pick):
        waiting.append((push(n, index, ref, mate), n, pick))

    def from_mate(limit=99):
        while waiting and limit:
            copy, n, pick = waiting.pop(0)
            copy.wait_recv()
            todo.append((n, 1 - core, pick))
            limit -= 1

    for n in (0, 1):
        for copy in stage1[n]:
            copy.wait_recv()
        axis = second[n]
        for side in (1, -1):
            flight[n, "line", side] = push(
                n, 8 + (side == 1), piece(n, core, here[lasts[n]], here[axis]), device(moved(axis, side), core))
        both_ways(n, "own", here[axis], 10)
    for copy in stage1[2]:
        copy.wait_recv()
    zwaves = {}
    for half in (0, 1):
        for side in (1, -1):
            zwaves[0, half, side] = push(
                2, 16 + half * 2 + (side == 1), zhalf(z, half), device(moved("z", side), core))
    to_mate(2, 40, plane(2, core, z), pick_plane(2, 0))

    recv_all(r_copy)
    factors = [jnp.where(lane < 64, r_buf[2 * pair], r_buf[2 * pair + 1]) for pair in range(8)]
    factors = jnp.concatenate(factors, axis=1)
    factors = jnp.concatenate([factors, factors], axis=0)
    digit_row = lax.broadcasted_iota(jnp.int32, (16, 1024), 0)
    table = jnp.zeros((16, 1024), F32)
    for digit, value in enumerate(split3(factors)):
        table = jnp.where(digit_row == digit, value, table)
    table = lax.dot_general(table.astype(BF16), onehot[...], (((1,), (1,)), ((), ())), preferred_element_type=F32)
    r_rows[...] = jnp.broadcast_to(table[0:1] + table[1:2] + table[2:3], r_rows.shape)

    def loaded(index, carry):
        head_copy(index).wait()
        return carry

    lax.fori_loop(0, 32, loaded, 0)

    def zstep(step):
        for half in (0, 1):
            for side in (1, -1):
                zwaves[step, half, side].wait_recv()
                at = moved("z", -side * (step + 1))["z"]
                if step < 2:
                    zwaves[step + 1, half, side] = push(
                        2, 16 + (step + 1) * 4 + half * 2 + (side == 1), zhalf(at, half), device(moved("z", side), core))
            if step == 2:
                zwaves[3, half, 2] = push(
                    2, 28 + half, zhalf(moved("z", -way * 3)["z"], half), device(moved("z", way), core))
        for side in (1, -1):
            by = -side * (step + 1)
            to_mate(2, 41 + step * 2 + (side == 1), plane(2, core, moved("z", by)["z"]), pick_plane(2, by))
            todo.append((2, core, pick_plane(2, by)))

    for n in (0, 1):
        axis = second[n]
        flight[n, "line", 1].wait_recv()
        flight[n, "line", -1].wait_recv()
        flight[n, "far"] = push(
            n, 12, piece(n, core, here[lasts[n]], moved(axis, -way)[axis]), device(moved(axis, way), core))
        both_ways(n, "left", moved(axis, -1)[axis], 13)
        both_ways(n, "right", moved(axis, 1)[axis], 15)
    zstep(0)
    for n in (0, 1):
        go_on(n, "own", here[second[n]], 17)
    todo.append((2, core, pick_plane(2, 0)))
    from_mate(1)
    work(2)
    for n in (0, 1):
        axis = second[n]
        flight[n, "far"].wait_recv()
        both_ways(n, "far", moved(axis, 2)[axis], 18)
        to_mate(n, 24, plane(n, core, here[lasts[n]]), pick_plane(n, 0))
        todo.append((n, core, pick_plane(n, 0)))
    zstep(1)
    work(2)
    for n in (0, 1):
        axis = second[n]
        go_on(n, "left", moved(axis, -1)[axis], 20)
        go_on(n, "right", moved(axis, 1)[axis], 21)
    zstep(2)
    from_mate(4)
    work(6)
    for n in (0, 1):
        axis = second[n]
        go_on(n, "far", moved(axis, 2)[axis], 22)
        for side in (1, -1):
            at = moved(lasts[n], side)[lasts[n]]
            to_mate(n, 25 + (side == 1), plane(n, core, at), pick_plane(n, side))
            todo.append((n, core, pick_plane(n, side)))
    from_mate(4)
    work()
    for half in (0, 1):
        zwaves[3, half, 2].wait_recv()
    to_mate(2, 47, plane(2, core, moved("z", 4)["z"]), pick_plane(2, 4))
    todo.append((2, core, pick_plane(2, 4)))
    for at, (name, by) in enumerate((("own", 0), ("left", -1), ("right", 1), ("far", 2))):
        for n in (0, 1):
            axis = second[n]
            b_at = moved(axis, by)[axis]
            flight[n, name, 2].wait_recv()
            c_at = moved(lasts[n], 2)[lasts[n]]
            to_mate(n, 27 + at, piece(n, core, c_at, b_at), pick_piece(n, 2, b_at))
            todo.append((n, core, pick_piece(n, 2, b_at)))
        from_mate(2)
        work()
    from_mate()
    work()

    lanes128 = lax.broadcasted_iota(jnp.int32, (64, 128), 1)
    lanes512 = lax.broadcasted_iota(jnp.int32, (64, 512), 1).astype(F32)

    def partials(block, carry):
        take = pl.ds(pl.multiple_of(block * 64, 64), 64)
        logits = acc[take, :]
        top = jnp.max(logits, axis=1, keepdims=True)
        low = logits - top
        expo = jnp.exp(low)
        total = jnp.sum(expo, axis=1, keepdims=True)
        cross = jnp.sum(expo * (low - st_rows[take, :].astype(F32)), axis=1, keepdims=True)
        pick = jnp.sum(jnp.where(lanes512 == id_cols[take, :], logits, 0.0), axis=1, keepdims=True)
        table = jnp.zeros((64, 128), F32)
        for at, value in enumerate((top, total, cross, pick)):
            for digit, part in enumerate(split3(value)):
                table = jnp.where(lanes128 == 8 * digit + at, part, table)
        stats[take, :] = table.astype(BF16)
        return carry

    lax.fori_loop(0, cap // 64, partials, 0)
    spread = lax.dot_general(stats[...], onehot[...], (((0,), (0,)), ((), ())), preferred_element_type=F32)
    spread = spread[0:8] + spread[8:16] + spread[16:24]
    for pair in range(8):
        fin_out[pair] = spread[:, 128 * pair:128 * (pair + 1)]
    start_all(fin_a_copy)
    fin_a[0] = fin_out[tok // 2]
    recv_all(fin_a_copy)

    def combine(ref):
        every = ref[...]
        top, total, cross, pick = (every[:, k:k + 1, :] for k in range(4))
        most = jnp.max(top, axis=0, keepdims=True)
        gap = top - most
        scale = jnp.exp(gap)
        return (most[0], jnp.sum(scale * total, axis=0), jnp.sum(scale * (cross + gap * total), axis=0),
                jnp.sum(pick, axis=0))

    sub = lax.broadcasted_iota(jnp.int32, (8, 128), 0)

    def table_of(values):
        table = jnp.zeros((8, 128), F32)
        for at, value in enumerate(values):
            table = jnp.where(sub == at, value, table)
        return table

    fin_b[0] = table_of(combine(fin_a))
    start_all(fin_b_copy)
    recv_all(fin_b_copy)
    top, total, cross, pick = combine(fin_b)
    log_total = jnp.log(total)
    kl = cross / total - log_total
    logprob = pick - (top + log_total)
    inside = jnp.where(lane < 64, lane, lane - 64)
    valid = inside < lens[tok]
    result = table_of((jnp.where(valid, kl, 0.0), jnp.where(valid, logprob, 0.0)))
    out[...] = jnp.where(tok % 2 == 0, result, pltpu.roll(result, 64, 1))

    for copy in sends:
        copy.wait_send()
    for copy in (sq_copy, a2a_copy, r_copy, fin_a_copy, fin_b_copy):
        sent_all(copy)


def run(groups, number, hidden, gain, lengths, ids, student, head):
    cap = 64 * sum(groups)
    hbm = pl.BlockSpec(memory_space=pl.ANY)
    return pl.pallas_call(
        functools.partial(kernel, groups),
        out_shape=jax.ShapeDtypeStruct((8, 128), F32),
        in_specs=[hbm, hbm, pl.BlockSpec(memory_space=pltpu.SMEM), hbm, hbm, hbm],
        out_specs=pl.BlockSpec(memory_space=pltpu.VMEM),
        scratch_shapes=[pltpu.VMEM((2, 4, 4, 8, 16 * count, 128), BF16) for count in groups] + [
            pltpu.VMEM((2, 4, 4, 8, 32, 512), BF16),
            pltpu.VMEM((1024, 512), BF16),
            pltpu.VMEM((64, 512), BF16),
            pltpu.VMEM((64, 128), F32),
            pltpu.VMEM((1, 1024), jnp.int32),
            pltpu.VMEM((cap, 1024), BF16),
            pltpu.VMEM((cap, 512), BF16),
            pltpu.VMEM((cap, 1), F32),
            pltpu.VMEM((cap, 512), F32),
            pltpu.VMEM((cap, 128), BF16),
            pltpu.VMEM((2, 4, 4, 8, 32, 128), F32),
            pltpu.VMEM((8, cap), F32),
            pltpu.VMEM((16, 8, 128), F32),
            pltpu.VMEM((16, 8, 128), F32),
            pltpu.VMEM((16, 32, 128), BF16),
            pltpu.VMEM((16, 32, 128), BF16),
            pltpu.VMEM((8, 8, 128), F32),
            pltpu.VMEM((16, 8, 128), F32),
            pltpu.VMEM((16, 8, 128), F32),
            pltpu.SemaphoreType.DMA((36,)),
            pltpu.SemaphoreType.DMA((10, 16)),
            pltpu.SemaphoreType.DMA((3, NMSG)),
            pltpu.SemaphoreType.DMA((3, NMSG)),
        ],
        compiler_params=pltpu.CompilerParams(
            collective_id=number, has_side_effects=True, vmem_limit_bytes=60 * 1024 * 1024),
        name="gathered_head_%d" % cap,
    )(hidden, gain, lengths, ids, student, head)


SPLITS = ((3, 3, 2), (6, 6, 4))


def per_device(hidden, gain, head_weight, student, token_ids, lengths):
    args = (hidden, gain.reshape(64, 128), lengths, token_ids.reshape(1, -1), student,
            head_weight.reshape(32, 8, 32, head_weight.shape[1]))
    if len(SPLITS) == 1:
        table = run(SPLITS[0], 0, *args)
    else:
        tokens = jnp.sum(lengths)
        which = sum((tokens > 64 * sum(groups)).astype(jnp.int32) for groups in SPLITS[:-1])
        table = lax.switch(which, [functools.partial(run, groups, at) for at, groups in enumerate(SPLITS)], *args)
    return table[0, :64], table[1, :64]


def solution(mesh):
    placed = (P("tok", "voc"), P(), P(None, ("tok", "voc")), P(None, ("tok", "voc")), P(), P())
    return jax.shard_map(
        per_device, mesh=mesh, in_specs=placed, out_specs=(P("tok"), P("tok")), check_vma=False
    )
```

```python
import functools

import jax
import jax.numpy as jnp
from jax import lax
from jax.experimental import pallas as pl
from jax.experimental.pallas import tpu as pltpu
from jax.sharding import PartitionSpec as P

D = 8192
LEN = 64
EPS = 1e-06
MESH = pl.DeviceIdType.MESH
F32 = jnp.float32
BF16 = jnp.bfloat16
RING = {"y": 4, "x": 4, "z": 8}
NMSG = 48
VALL = slice(None)


def split3(value):
    hi = value.astype(BF16).astype(F32)
    rest = value - hi
    mid = rest.astype(BF16).astype(F32)
    return hi, mid, (rest - mid).astype(BF16).astype(F32)


def blocks_of(groups):
    blocks = [[] for _ in groups]
    start = 0
    for part, count in enumerate(groups):
        for _ in range(count // 2):
            blocks[part].append((start, 128))
            start += 128
    for part, count in enumerate(groups):
        if count % 2:
            blocks[part].append((start, 64))
            start += 64
    return blocks


def kernel(groups, hidden, gain, lens, ids, student, head, out, *scratch):
    cap = (sum(groups) + 1) // 2 * 128
    blocks = blocks_of(groups)
    lasts = ("x", "y", "z")
    slabs = scratch[:3]
    (w_all, st_all, h_in, gain_in, ids_in, onehot, st_rows, id_cols, acc, stats, gcol, r_rows, sq_buf, r_buf, a2a_out,
     a2a_in, fin_out, fin_a, fin_b, local_sem, pair_sem, send_sem, recv_sem) = scratch[3:]
    tok = lax.axis_index("tok")
    voc = lax.axis_index("voc")
    here = {"y": (voc // 8) * 2 + tok // 8, "x": (voc // 2) % 4, "z": tok % 8}
    core = voc % 2
    way = 1 - 2 * core

    def device(place, which):
        return {"tok": (place["y"] % 2) * 8 + place["z"], "voc": ((place["y"] // 2) * 4 + place["x"]) * 2 + which}

    def moved(axis, by):
        place = dict(here)
        place[axis] = lax.rem(here[axis] + by + RING[axis], RING[axis])
        return place

    def tok_peer(step):
        return {"tok": lax.rem(tok + step, 16), "voc": voc}

    def voc_peer(step):
        return {"tok": tok, "voc": lax.rem(voc + step, 16)}

    def plane_peer(step):
        return device({"y": lax.rem(here["y"] + step // 4, 4), "x": lax.rem(here["x"] + step % 4, 4), "z": here["z"]}, core)

    hidden_copy = pltpu.make_async_copy(hidden, h_in, local_sem.at[0])
    hidden_copy.start()
    barrier = pltpu.get_barrier_semaphore()

    def greet(step, carry):
        pl.semaphore_signal(barrier, inc=1, device_id=tok_peer(step), device_id_type=MESH)
        pl.semaphore_signal(barrier, inc=1, device_id=voc_peer(step), device_id_type=MESH)
        return carry

    lax.fori_loop(1, 16, greet, 0)
    for step in range(4, 16):
        dy, dx = step // 4, step % 4
        if dy % 2 and dx:
            pl.semaphore_signal(barrier, inc=1, device_id=plane_peer(step), device_id_type=MESH)
    across = {"tok": lax.rem(tok + 8, 16), "voc": lax.rem(voc + 8, 16)}
    pl.semaphore_signal(barrier, inc=1, device_id=across, device_id_type=MESH)

    def head_copy(index):
        y = (index // 16) * 2 + index % 2
        return pltpu.make_async_copy(
            head.at[index], w_all.at[(index // 2) % 2, y, (index // 4) % 4], local_sem.at[4]
        )

    gain_copy = pltpu.make_async_copy(gain, gain_in, local_sem.at[1])
    ids_copy = pltpu.make_async_copy(ids, ids_in, local_sem.at[2])
    student_copy = pltpu.make_async_copy(student, st_all, local_sem.at[3])
    hidden_copy.wait()
    rows = h_in[...].astype(F32)
    rows = jnp.concatenate([rows, rows], axis=0)
    turned = rows.T
    square = jnp.sum(turned * turned, axis=0, keepdims=True)
    sq_buf[0] = square
    lane = lax.broadcasted_iota(jnp.int32, (1, 128), 1)
    turned = turned.reshape(16, 32, 128)
    a2a_out[...] = jnp.where(lane[None] < 64, turned[:, 0:16], turned[:, 16:32]).astype(BF16)

    pl.semaphore_wait(barrier, 37)

    def sq_copy(step):
        return pltpu.make_async_remote_copy(
            src_ref=sq_buf.at[0], dst_ref=sq_buf.at[step], send_sem=pair_sem.at[0],
            recv_sem=pair_sem.at[1], device_id=voc_peer(step), device_id_type=MESH)

    def a2a_copy(step):
        return pltpu.make_async_remote_copy(
            src_ref=a2a_out.at[lax.rem(tok + step, 16)], dst_ref=a2a_in.at[tok], send_sem=pair_sem.at[2],
            recv_sem=pair_sem.at[3], device_id=tok_peer(step), device_id_type=MESH)

    def r_copy(step):
        return pltpu.make_async_remote_copy(
            src_ref=r_buf.at[tok], dst_ref=r_buf.at[tok], send_sem=pair_sem.at[8],
            recv_sem=pair_sem.at[9], device_id=tok_peer(step), device_id_type=MESH)

    def fin_a_copy(step):
        return pltpu.make_async_remote_copy(
            src_ref=fin_out.at[lax.rem(tok + step, 16)], dst_ref=fin_a.at[step], send_sem=pair_sem.at[4],
            recv_sem=pair_sem.at[5], device_id=tok_peer(step), device_id_type=MESH)

    def fin_b_copy(step):
        return pltpu.make_async_remote_copy(
            src_ref=fin_b.at[0], dst_ref=fin_b.at[step], send_sem=pair_sem.at[6],
            recv_sem=pair_sem.at[7], device_id=voc_peer(step), device_id_type=MESH)

    def start_all(copy):
        def body(step, carry):
            copy(step).start()
            return carry
        lax.fori_loop(1, 16, body, 0)

    def group(ref, first, at):
        view = ref.at[pl.ds(first, 15)]
        return pltpu.make_async_remote_copy(
            src_ref=view, dst_ref=view, send_sem=pair_sem.at[at], recv_sem=pair_sem.at[at + 1],
            device_id=tok_peer(1), device_id_type=MESH)

    sq_group, a2a_group, r_group = group(sq_buf, 1, 0), group(a2a_in, 0, 2), group(r_buf, 0, 8)
    fin_a_group, fin_b_group = group(fin_a, 1, 4), group(fin_b, 1, 6)

    start_all(a2a_copy)
    start_all(sq_copy)
    a2a_in[tok] = a2a_out[tok]

    gain_copy.start()
    ids_copy.start()
    student_copy.start()

    def load(index, carry):
        head_copy(index).start()
        return carry

    lax.fori_loop(0, 32, load, 0)

    place_of = []
    offset = jnp.int32(0)
    for pair in range(8):
        first, second = lens[2 * pair], lens[2 * pair + 1]
        low = jnp.where(lane < first, offset + lane, -1)
        high = jnp.where(lane - 64 < second, offset + first + lane - 64, -1)
        place_of.append(jnp.where(lane < 64, low, high))
        offset = offset + first + second
    place_of = jnp.concatenate(place_of, axis=1)

    def fill(block, carry):
        start = pl.multiple_of(block * 64, 64)
        want = lax.broadcasted_iota(jnp.int32, (64, 1024), 0) + start
        onehot[pl.ds(start, 64), :] = jnp.where(want == place_of, 1.0, 0.0).astype(BF16)
        return carry

    lax.fori_loop(0, cap // 64, fill, 0)


    a2a_group.wait_recv()
    pieces = []
    for pair in range(8):
        low, high = a2a_in[2 * pair].astype(F32), a2a_in[2 * pair + 1].astype(F32)
        upper = jnp.where(lane < 64, low, pltpu.roll(high, 64, 1))
        under = jnp.where(lane < 64, pltpu.roll(low, 64, 1), high)
        pieces.append(jnp.concatenate([upper, under], axis=0))
    block = jnp.concatenate(pieces, axis=1).astype(BF16)
    packed = lax.dot_general(block, onehot[...], (((1,), (1,)), ((), ())), preferred_element_type=F32)

    numbers = {}

    def number_of(*key):
        return numbers.setdefault(key, len(numbers))

    def push(n, sent, key, src, target):
        pltpu.make_async_remote_copy(
            src_ref=src, dst_ref=src, send_sem=send_sem.at[3 * n + sent], recv_sem=recv_sem.at[number_of(n, *key)],
            device_id=target, device_id_type=MESH).start()

    def arrive(n, key, view):
        pltpu.make_async_remote_copy(
            src_ref=view, dst_ref=view, send_sem=send_sem.at[0], recv_sem=recv_sem.at[number_of(n, *key)],
            device_id=mate, device_id_type=MESH).wait_recv()

    mate = device(here, 1 - core)
    y, x, z = here["y"], here["x"], here["z"]
    own = [slab.at[core, y, x, z] for slab in slabs]
    for n in range(3):
        for at, (start, wide) in enumerate(blocks[n]):
            if wide == 128:
                slabs[n][core, y, x, z, 32 * at:32 * at + 32] = packed[:, start:start + 128].astype(BF16)
            else:
                base = start // 128 * 128
                both = packed[:, base:base + 128]
                flipped = pltpu.roll(both, 64, 1)
                if start == base:
                    half = jnp.where(lane < 64, both[0:16], flipped[16:32])
                else:
                    half = jnp.where(lane < 64, flipped[0:16], both[16:32])
                slabs[n][core, y, x, z, 32 * at:32 * at + 16] = half.astype(BF16)
        if n < 2:
            for by in (4, 3, 5, 2, 6, 1, 7):
                push(n, 0, ("first",), own[n], device(moved("z", by), core))
        else:
            for step in (10, 2, 8, 6, 9, 11, 14, 1, 3, 4, 12, 5, 7, 13, 15):
                push(n, 0, ("first",), own[n], plane_peer(step))
    firsts = [slabs[0].at[core, y, x, pl.ds(0, 7)], slabs[1].at[core, y, x, pl.ds(0, 7)],
              slabs[2].at[core, pl.ds(0, 3), 0, pl.ds(0, 5)]]
    sent_views = []
    for n in (0, 1):
        sent_views += [firsts[n], slabs[n].at[0], slabs[n].at[:, :, pl.ds(0, 3), pl.ds(0, 5)]]
    sent_views += [firsts[2], slabs[2].at[0, :, :, pl.ds(0, 7)], slabs[2].at[0]]

    sq_group.wait_recv()
    total_sq = sq_buf[0]
    for step in range(1, 16):
        total_sq = total_sq + sq_buf[step]
    r_buf[tok] = lax.rsqrt(total_sq / D + EPS)
    start_all(r_copy)

    gain_copy.wait()

    def spread_gain(row, carry):
        wide = jnp.broadcast_to(gain_in[pl.ds(row, 1), :], (128, 128)).T
        index = row // 2
        y = (index // 16) * 2 + index % 2
        start = pl.multiple_of((row % 2) * 4, 4)
        gcol[(index // 2) % 2, y, (index // 4) % 4, pl.ds(start, 4)] = wide.reshape(4, 32, 128)
        return carry

    lax.fori_loop(0, 64, spread_gain, 0)

    def zero(block, carry):
        acc[pl.ds(pl.multiple_of(block * 64, 64), 64), :] = jnp.zeros((64, 512), F32)
        return carry

    lax.fori_loop(0, cap // 64, zero, 0)

    def piece(n, which, c_at, b_at):
        if n == 0:
            return slabs[0].at[which, b_at, c_at]
        return slabs[1].at[which, c_at, b_at]

    def plane(n, which, c_at):
        if n == 0:
            return slabs[0].at[which, :, c_at]
        if n == 1:
            return slabs[1].at[which, c_at]
        return slabs[2].at[which, :, :, c_at]

    def zhalf(c_at, half):
        return slabs[2].at[core, pl.ds(2 * half, 2), :, c_at]

    second = ("y", "x")

    def two_lines(n):
        return slabs[0].at[core, pl.ds(0, 2), x] if n == 0 else slabs[1].at[core, y, pl.ds(0, 2)]

    def two_planes(n, which):
        if n == 0:
            return slabs[0].at[which, :, pl.ds(0, 2)]
        if n == 1:
            return slabs[1].at[which, pl.ds(0, 2)]
        return slabs[2].at[which, :, :, pl.ds(0, 2)]

    def both_ways(n, name, b_at):
        axis = lasts[n]
        for side in (1, -1):
            push(n, 1, (name,), piece(n, core, here[axis], b_at), device(moved(axis, side), core))

    def go_on(n, name, b_at):
        axis = lasts[n]
        arrive(n, (name,), two_lines(n))
        push(n, 2, (name, "on"), piece(n, core, moved(axis, -way)[axis], b_at), device(moved(axis, way), core))

    def multiply(n, which, pick):
        weight = gcol[(which, *pick)].reshape(-1, 128)
        depth = weight.shape[0]
        lefts = []
        for at, (start, wide) in enumerate(blocks[n]):
            base = start // 128 * 128
            factor = r_rows[0:1, base:base + 128]
            if wide == 128:
                left = slabs[n][(which, *pick, slice(32 * at, 32 * at + 32))].astype(F32).reshape(depth, 128)
            else:
                left = slabs[n][(which, *pick, slice(32 * at, 32 * at + 16))].astype(F32).reshape(depth // 32, 16, 128)
                left = jnp.concatenate([left, pltpu.roll(left, 64, 2)], axis=1).reshape(depth, 128)
                if start != base:
                    factor = pltpu.roll(factor, 64, 1)
            lefts.append((left * factor * weight).astype(BF16)[:, :wide])
        left = jnp.concatenate(lefts, axis=1) if len(lefts) > 1 else lefts[0]
        right = w_all[(which, *pick)].reshape(depth, 512)
        term = lax.dot_general(left, right, (((0,), (0,)), ((), ())), preferred_element_type=F32)
        row = 0
        for start, wide in blocks[n]:
            acc[start:start + wide, :] += term[row:row + wide]
            row += wide

    def pick_plane(n, by):
        axis = lasts[n]
        at = moved(axis, by)[axis]
        return tuple(at if axis == name else VALL for name in ("y", "x", "z"))

    def pick_piece(n, by, b_at):
        axis = lasts[n]
        at = moved(axis, by)[axis]
        return (b_at, at, VALL) if n == 0 else (at, b_at, VALL)

    todo = []

    def work(limit=99):
        while todo and limit:
            multiply(*todo.pop(0))
            limit -= 1

    waiting = []

    def to_mate(n, sent, key, refs, view, picks):
        for ref in refs:
            push(n, sent, ("mate", *key), ref, mate)
        waiting.append((n, ("mate", *key), view, picks))

    def from_mate(limit=99):
        while waiting and limit:
            n, key, view, picks = waiting.pop(0)
            arrive(n, key, view)
            todo.extend((n, 1 - core, pick) for pick in picks)
            limit -= 1

    for n in (0, 1):
        arrive(n, ("first",), firsts[n])
        axis = second[n]
        for side in (1, -1):
            push(n, 2, ("line",), piece(n, core, here[lasts[n]], here[axis]), device(moved(axis, side), core))
    for n in (0, 1):
        both_ways(n, "own", here[second[n]])
    arrive(2, ("first",), firsts[2])
    for half in (0, 1):
        for side in (1, -1):
            push(2, 1, ("wave", 0, half), zhalf(z, half), device(moved("z", side), core))
    to_mate(2, 2, (0,), [plane(2, core, z)], plane(2, 1 - core, z), [pick_plane(2, 0)])

    r_group.wait_recv()
    factors = [jnp.where(lane < 64, r_buf[2 * pair], r_buf[2 * pair + 1]) for pair in range(8)]
    factors = jnp.concatenate(factors, axis=1)
    factors = jnp.broadcast_to(factors, (16, 1024))
    digit_row = lax.broadcasted_iota(jnp.int32, (16, 1024), 0)
    table = jnp.zeros((16, 1024), F32)
    for digit, value in enumerate(split3(factors)):
        table = jnp.where(digit_row == digit, value, table)
    table = lax.dot_general(table.astype(BF16), onehot[...], (((1,), (1,)), ((), ())), preferred_element_type=F32)
    r_rows[...] = jnp.broadcast_to(table[0:1] + table[1:2] + table[2:3], r_rows.shape)

    pltpu.make_async_copy(w_all, w_all, local_sem.at[4]).wait()

    def zstep(step):
        for half in (0, 1):
            arrive(2, ("wave", step, half), slabs[2].at[core, pl.ds(0, 2), :, pl.ds(0, 2)])
            for side in (1, -1):
                at = moved("z", -side * (step + 1))["z"]
                if step < 2:
                    push(2, 1, ("wave", step + 1, half), zhalf(at, half), device(moved("z", side), core))
            if step == 2:
                push(2, 1, ("wave", 3, half), zhalf(moved("z", -way * 3)["z"], half), device(moved("z", way), core))
        sides = (step + 1, -step - 1)
        picks = [pick_plane(2, by) for by in sides]
        to_mate(2, 2, (step + 1,), [plane(2, core, moved("z", by)["z"]) for by in sides], two_planes(2, 1 - core), picks)
        todo.extend((2, core, pick) for pick in picks)

    ids_copy.wait()
    local_id = ids_in[...] - (tok * 16 + voc) * 512
    local_id = jnp.where((local_id >= 0) & (local_id < 512), local_id, 512)
    digits = jnp.where(lax.broadcasted_iota(jnp.int32, (16, 1024), 0) == 0, local_id // 256, local_id % 256)
    digits = digits.astype(F32).astype(BF16)
    cols = lax.dot_general(onehot[...], digits, (((1,), (1,)), ((), ())), preferred_element_type=F32)
    id_cols[...] = cols[:, 0:1] * 256.0 + cols[:, 1:2]
    student_copy.wait()
    st_rows[...] = jnp.dot(onehot[...], st_all[...], preferred_element_type=F32).astype(BF16)

    todo.append((2, core, pick_plane(2, 0)))
    work()
    for n in (0, 1):
        axis = second[n]
        arrive(n, ("line",), two_lines(n))
        push(n, 2, ("opposite",), piece(n, core, here[lasts[n]], moved(axis, -way)[axis]), device(moved(axis, way), core))
    for n in (0, 1):
        axis = second[n]
        both_ways(n, "left", moved(axis, -1)[axis])
        both_ways(n, "right", moved(axis, 1)[axis])
    zstep(0)
    for n in (0, 1):
        go_on(n, "own", here[second[n]])
    from_mate(1)
    work(2)
    for n in (0, 1):
        axis = second[n]
        arrive(n, ("opposite",), piece(n, core, here[lasts[n]], 0))
        both_ways(n, "far", moved(axis, 2)[axis])
    for n in (0, 1):
        at = here[lasts[n]]
        to_mate(n, 2, (0,), [plane(n, core, at)], plane(n, 1 - core, at), [pick_plane(n, 0)])
        todo.append((n, core, pick_plane(n, 0)))
    zstep(1)
    work(2)

    def opposite(n, name, by):
        axis = second[n]
        b_at = moved(axis, by)[axis]
        arrive(n, (name, "on"), piece(n, core, here[lasts[n]], 0))
        c_at = moved(lasts[n], 2)[lasts[n]]
        ref, other = piece(n, core, c_at, b_at), piece(n, 1 - core, c_at, b_at)
        to_mate(n, 2, (name,), [ref], other, [pick_piece(n, 2, b_at)])
        todo.append((n, core, pick_piece(n, 2, b_at)))

    for n in (0, 1):
        go_on(n, "left", moved(second[n], -1)[second[n]])
    for n in (0, 1):
        go_on(n, "right", moved(second[n], 1)[second[n]])
    for n in (0, 1):
        opposite(n, "own", 0)
    work(2)
    zstep(2)
    from_mate(4)
    work(4)
    for n in (0, 1):
        go_on(n, "far", moved(second[n], 2)[second[n]])
    for n in (0, 1):
        picks = [pick_plane(n, side) for side in (1, -1)]
        places = [moved(lasts[n], side)[lasts[n]] for side in (1, -1)]
        to_mate(n, 1, (1,), [plane(n, core, at) for at in places], two_planes(n, 1 - core), picks)
        todo.extend((n, core, pick) for pick in picks)
    work(4)
    for n in (0, 1):
        opposite(n, "left", -1)
    for n in (0, 1):
        opposite(n, "right", 1)
    from_mate(3)
    work(4)
    for half in (0, 1):
        arrive(2, ("wave", 3, half), zhalf(z, 0))
    at = moved("z", 4)["z"]
    to_mate(2, 2, (4,), [plane(2, core, at)], plane(2, 1 - core, at), [pick_plane(2, 4)])
    todo.append((2, core, pick_plane(2, 4)))
    for n in (0, 1):
        opposite(n, "far", 2)
    work()
    from_mate()
    work()

    lanes128 = lax.broadcasted_iota(jnp.int32, (64, 128), 1)
    lanes512 = lax.broadcasted_iota(jnp.int32, (64, 512), 1).astype(F32)

    def partials(block):
        take = pl.ds(block * 64, 64)
        logits = acc[take, :]
        top = jnp.max(logits, axis=1, keepdims=True)
        low = logits - top
        expo = jnp.exp(low)
        total = jnp.sum(expo, axis=1, keepdims=True)
        cross = jnp.sum(expo * (low - st_rows[take, :].astype(F32)), axis=1, keepdims=True)
        pick = jnp.sum(jnp.where(lanes512 == id_cols[take, :], logits, 0.0), axis=1, keepdims=True)
        table = jnp.zeros((64, 128), F32)
        for at, value in enumerate((top, total, cross, pick)):
            for digit, part in enumerate(split3(value)):
                table = jnp.where(lanes128 == 8 * digit + at, part, table)
        stats[take, :] = table.astype(BF16)

    assert len(numbers) == NMSG, len(numbers)
    for block in range(cap // 64):
        partials(block)
    spread = lax.dot_general(stats[...], onehot[...], (((0,), (0,)), ((), ())), preferred_element_type=F32)
    spread = spread[0:8] + spread[8:16] + spread[16:24]
    for pair in range(8):
        rows4 = spread[:, 128 * pair:128 * (pair + 1)]
        turned4 = pltpu.roll(rows4, 64, 1)
        fin_out[2 * pair] = jnp.where(lane < 64, rows4[0:2], turned4[2:4])
        fin_out[2 * pair + 1] = jnp.where(lane < 64, turned4[0:2], rows4[2:4])
    start_all(fin_a_copy)
    fin_a[0] = fin_out[tok]
    for at, view in enumerate(sent_views):
        pltpu.make_async_remote_copy(
            src_ref=view, dst_ref=view, send_sem=send_sem.at[at], recv_sem=recv_sem.at[0], device_id=mate,
            device_id_type=MESH).wait_send()
    for copies in (sq_group, a2a_group, r_group):
        copies.wait_send()
    fin_a_group.wait_recv()

    def combine(ref):
        every = ref[...]
        top, total = every[:, 0:1, :], every[:, 1:2, :]
        cross, pick = pltpu.roll(top, 64, 2), pltpu.roll(total, 64, 2)
        most = jnp.max(top, axis=0, keepdims=True)
        gap = top - most
        scale = jnp.exp(gap)
        return (most[0], jnp.sum(scale * total, axis=0), jnp.sum(scale * (cross + gap * total), axis=0),
                jnp.sum(pick, axis=0))

    sub = lax.broadcasted_iota(jnp.int32, (8, 128), 0)

    def table_of(values):
        table = jnp.zeros((8, 128), F32)
        for at, value in enumerate(values):
            table = jnp.where(sub == at, value, table)
        return table

    top, total, cross, pick = combine(fin_a)
    fin_b[0] = jnp.concatenate(
        [jnp.where(lane < 64, top, pltpu.roll(cross, 64, 1)), jnp.where(lane < 64, total, pltpu.roll(pick, 64, 1))], axis=0)
    start_all(fin_b_copy)
    fin_b_group.wait_recv()
    top, total, cross, pick = combine(fin_b)
    log_total = jnp.log(total)
    kl = cross / total - log_total
    logprob = pick - (top + log_total)
    valid = lane < lens[tok]
    out[...] = table_of((jnp.where(valid, kl, 0.0), jnp.where(valid, logprob, 0.0)))
    fin_a_group.wait_send()
    fin_b_group.wait_send()


def run(groups, number, hidden, gain, lengths, ids, student, head):
    cap = (sum(groups) + 1) // 2 * 128
    hbm = pl.BlockSpec(memory_space=pl.ANY)
    return pl.pallas_call(
        functools.partial(kernel, groups),
        out_shape=jax.ShapeDtypeStruct((8, 128), F32),
        in_specs=[hbm, hbm, pl.BlockSpec(memory_space=pltpu.SMEM), hbm, hbm, hbm],
        out_specs=pl.BlockSpec(memory_space=pltpu.VMEM),
        scratch_shapes=[pltpu.VMEM((2, 4, 4, 8, 16 * count, 128), BF16) for count in groups] + [
            pltpu.VMEM((2, 4, 4, 8, 32, 512), BF16),
            pltpu.VMEM((1024, 512), BF16),
            pltpu.VMEM((64, 512), BF16),
            pltpu.VMEM((64, 128), F32),
            pltpu.VMEM((1, 1024), jnp.int32),
            pltpu.VMEM((cap, 1024), BF16),
            pltpu.VMEM((cap, 512), BF16),
            pltpu.VMEM((cap, 1), F32),
            pltpu.VMEM((cap, 512), F32),
            pltpu.VMEM((cap, 128), BF16),
            pltpu.VMEM((2, 4, 4, 8, 32, 128), F32),
            pltpu.VMEM((8, cap), F32),
            pltpu.VMEM((16, 1, 128), F32),
            pltpu.VMEM((16, 1, 128), F32),
            pltpu.VMEM((16, 16, 128), BF16),
            pltpu.VMEM((16, 16, 128), BF16),
            pltpu.VMEM((16, 2, 128), F32),
            pltpu.VMEM((16, 2, 128), F32),
            pltpu.VMEM((16, 2, 128), F32),
            pltpu.SemaphoreType.DMA((5,)),
            pltpu.SemaphoreType.DMA((10,)),
            pltpu.SemaphoreType.DMA((9,)),
            pltpu.SemaphoreType.DMA((NMSG,)),
        ],
        compiler_params=pltpu.CompilerParams(
            collective_id=number, has_side_effects=True, vmem_limit_bytes=60 * 1024 * 1024),
        name="gathered_head_%d" % (64 * sum(groups)),
    )(hidden, gain, lengths, ids, student, head)


SPLITS = ((3, 3, 2), (3, 3, 3), (4, 4, 2), (6, 6, 4))


def per_device(hidden, gain, head_weight, student, token_ids, lengths):
    args = (hidden, gain.reshape(64, 128), lengths, token_ids.reshape(1, -1), student,
            head_weight.reshape(32, 8, 32, head_weight.shape[1]))
    if len(SPLITS) == 1:
        table = run(SPLITS[0], 0, *args)
    else:
        tokens = jnp.sum(lengths)
        which = sum((tokens > 64 * sum(groups)).astype(jnp.int32) for groups in SPLITS[:-1])
        table = lax.switch(which, [functools.partial(run, groups, at) for at, groups in enumerate(SPLITS)], *args)
    return table[0, :64], table[1, :64]


def solution(mesh):
    placed = (P("tok", "voc"), P(), P(None, ("tok", "voc")), P(None, ("tok", "voc")), P(), P())
    return jax.shard_map(
        per_device, mesh=mesh, in_specs=placed, out_specs=(P("tok"), P("tok")), check_vma=False
    )
```

```python
import functools

import jax
import jax.numpy as jnp
from jax import lax
from jax.experimental import pallas as pl
from jax.experimental.pallas import tpu as pltpu
from jax.sharding import PartitionSpec as P

D = 8192
LEN = 64
EPS = 1e-06
MESH = pl.DeviceIdType.MESH
F32 = jnp.float32
BF16 = jnp.bfloat16
RING = {"y": 4, "x": 4, "z": 8}
NMSG = 44
VALL = slice(None)


def split3(value):
    hi = value.astype(BF16).astype(F32)
    rest = value - hi
    mid = rest.astype(BF16).astype(F32)
    return hi, mid, (rest - mid).astype(BF16).astype(F32)


def blocks_of(groups):
    blocks = [[] for _ in groups]
    start = 0
    for part, count in enumerate(groups):
        for _ in range(count // 2):
            blocks[part].append((start, 128))
            start += 128
    for part, count in enumerate(groups):
        if count % 2:
            blocks[part].append((start, 64))
            start += 64
    return blocks


def kernel(groups, hidden, gain, lens, ids, student, head, out, *scratch):
    cap = (sum(groups) + 1) // 2 * 128
    blocks = blocks_of(groups)
    lasts = ("x", "y", "z")
    slabs = scratch[:3]
    (w_all, st_all, h_in, gain_in, ids_in, onehot, st_rows, id_cols, acc, stats, gcol, r_rows, sq_buf, r_buf, a2a_out,
     a2a_in, fin_out, fin_a, fin_b, local_sem, pair_sem, send_sem, recv_sem) = scratch[3:]
    tok = lax.axis_index("tok")
    voc = lax.axis_index("voc")
    here = {"y": (voc // 8) * 2 + tok // 8, "x": (voc // 2) % 4, "z": tok % 8}
    core = voc % 2
    way = 1 - 2 * core

    def device(place, which):
        return {"tok": (place["y"] % 2) * 8 + place["z"], "voc": ((place["y"] // 2) * 4 + place["x"]) * 2 + which}

    def moved(axis, by):
        place = dict(here)
        place[axis] = lax.rem(here[axis] + by + RING[axis], RING[axis])
        return place

    def tok_peer(step):
        return {"tok": lax.rem(tok + step, 16), "voc": voc}

    def voc_peer(step):
        return {"tok": tok, "voc": lax.rem(voc + step, 16)}

    def plane_peer(step):
        return device({"y": lax.rem(here["y"] + step // 4, 4), "x": lax.rem(here["x"] + step % 4, 4), "z": here["z"]}, core)

    hidden_copy = pltpu.make_async_copy(hidden, h_in, local_sem.at[0])
    hidden_copy.start()
    barrier = pltpu.get_barrier_semaphore()

    def greet(step, carry):
        pl.semaphore_signal(barrier, inc=1, device_id=tok_peer(step), device_id_type=MESH)
        pl.semaphore_signal(barrier, inc=1, device_id=voc_peer(step), device_id_type=MESH)
        return carry

    lax.fori_loop(1, 16, greet, 0)
    for step in range(4, 16):
        dy, dx = step // 4, step % 4
        if dy % 2 and dx:
            pl.semaphore_signal(barrier, inc=1, device_id=plane_peer(step), device_id_type=MESH)
    across = {"tok": lax.rem(tok + 8, 16), "voc": lax.rem(voc + 8, 16)}
    pl.semaphore_signal(barrier, inc=1, device_id=across, device_id_type=MESH)

    def head_copy(index):
        y = (index // 16) * 2 + index % 2
        return pltpu.make_async_copy(
            head.at[index], w_all.at[(index // 2) % 2, y, (index // 4) % 4], local_sem.at[4]
        )

    gain_copy = pltpu.make_async_copy(gain, gain_in, local_sem.at[1])
    ids_copy = pltpu.make_async_copy(ids, ids_in, local_sem.at[2])
    student_copy = pltpu.make_async_copy(student, st_all, local_sem.at[3])
    hidden_copy.wait()
    rows = h_in[...].astype(F32)
    rows = jnp.concatenate([rows, rows], axis=0)
    turned = rows.T
    square = jnp.sum(turned * turned, axis=0, keepdims=True)
    sq_buf[0] = square
    lane = lax.broadcasted_iota(jnp.int32, (1, 128), 1)
    turned = turned.reshape(16, 32, 128)
    a2a_out[...] = jnp.where(lane[None] < 64, turned[:, 0:16], turned[:, 16:32]).astype(BF16)

    pl.semaphore_wait(barrier, 37)

    def sq_copy(step):
        return pltpu.make_async_remote_copy(
            src_ref=sq_buf.at[0], dst_ref=sq_buf.at[step], send_sem=pair_sem.at[0],
            recv_sem=pair_sem.at[1], device_id=voc_peer(step), device_id_type=MESH)

    def a2a_copy(step):
        return pltpu.make_async_remote_copy(
            src_ref=a2a_out.at[lax.rem(tok + step, 16)], dst_ref=a2a_in.at[tok], send_sem=pair_sem.at[2],
            recv_sem=pair_sem.at[3], device_id=tok_peer(step), device_id_type=MESH)

    def r_copy(step):
        return pltpu.make_async_remote_copy(
            src_ref=r_buf.at[tok], dst_ref=r_buf.at[tok], send_sem=pair_sem.at[8],
            recv_sem=pair_sem.at[9], device_id=tok_peer(step), device_id_type=MESH)

    def fin_a_copy(step):
        return pltpu.make_async_remote_copy(
            src_ref=fin_out.at[lax.rem(tok + step, 16)], dst_ref=fin_a.at[step], send_sem=pair_sem.at[4],
            recv_sem=pair_sem.at[5], device_id=tok_peer(step), device_id_type=MESH)

    def fin_b_copy(step):
        return pltpu.make_async_remote_copy(
            src_ref=fin_b.at[0], dst_ref=fin_b.at[step], send_sem=pair_sem.at[6],
            recv_sem=pair_sem.at[7], device_id=voc_peer(step), device_id_type=MESH)

    def start_all(copy):
        def body(step, carry):
            copy(step).start()
            return carry
        lax.fori_loop(1, 16, body, 0)

    def group(ref, first, at):
        view = ref.at[pl.ds(first, 15)]
        return pltpu.make_async_remote_copy(
            src_ref=view, dst_ref=view, send_sem=pair_sem.at[at], recv_sem=pair_sem.at[at + 1],
            device_id=tok_peer(1), device_id_type=MESH)

    sq_group, a2a_group, r_group = group(sq_buf, 1, 0), group(a2a_in, 0, 2), group(r_buf, 0, 8)
    fin_a_group, fin_b_group = group(fin_a, 1, 4), group(fin_b, 1, 6)

    start_all(a2a_copy)
    start_all(sq_copy)
    a2a_in[tok] = a2a_out[tok]

    gain_copy.start()
    ids_copy.start()
    student_copy.start()

    def load(index, carry):
        head_copy(index).start()
        return carry

    lax.fori_loop(0, 32, load, 0)

    place_of = []
    offset = jnp.int32(0)
    for pair in range(8):
        first, second = lens[2 * pair], lens[2 * pair + 1]
        low = jnp.where(lane < first, offset + lane, -1)
        high = jnp.where(lane - 64 < second, offset + first + lane - 64, -1)
        place_of.append(jnp.where(lane < 64, low, high))
        offset = offset + first + second
    place_of = jnp.concatenate(place_of, axis=1)

    def fill(block, carry):
        start = pl.multiple_of(block * 64, 64)
        want = lax.broadcasted_iota(jnp.int32, (64, 1024), 0) + start
        onehot[pl.ds(start, 64), :] = jnp.where(want == place_of, 1.0, 0.0).astype(BF16)
        return carry

    lax.fori_loop(0, cap // 64, fill, 0)


    a2a_group.wait_recv()
    pieces = []
    for pair in range(8):
        low, high = a2a_in[2 * pair].astype(F32), a2a_in[2 * pair + 1].astype(F32)
        upper = jnp.where(lane < 64, low, pltpu.roll(high, 64, 1))
        under = jnp.where(lane < 64, pltpu.roll(low, 64, 1), high)
        pieces.append(jnp.concatenate([upper, under], axis=0))
    block = jnp.concatenate(pieces, axis=1).astype(BF16)
    packed = lax.dot_general(block, onehot[...], (((1,), (1,)), ((), ())), preferred_element_type=F32)

    numbers = {}

    def number_of(*key):
        return numbers.setdefault(key, len(numbers))

    def push(n, sent, key, src, target):
        pltpu.make_async_remote_copy(
            src_ref=src, dst_ref=src, send_sem=send_sem.at[3 * n + sent], recv_sem=recv_sem.at[number_of(n, *key)],
            device_id=target, device_id_type=MESH).start()

    def arrive(n, key, view):
        pltpu.make_async_remote_copy(
            src_ref=view, dst_ref=view, send_sem=send_sem.at[0], recv_sem=recv_sem.at[number_of(n, *key)],
            device_id=mate, device_id_type=MESH).wait_recv()

    mate = device(here, 1 - core)
    y, x, z = here["y"], here["x"], here["z"]
    own = [slab.at[core, y, x, z] for slab in slabs]
    for n in range(3):
        for at, (start, wide) in enumerate(blocks[n]):
            if wide == 128:
                slabs[n][core, y, x, z, 32 * at:32 * at + 32] = packed[:, start:start + 128].astype(BF16)
            else:
                base = start // 128 * 128
                both = packed[:, base:base + 128]
                flipped = pltpu.roll(both, 64, 1)
                if start == base:
                    half = jnp.where(lane < 64, both[0:16], flipped[16:32])
                else:
                    half = jnp.where(lane < 64, flipped[0:16], both[16:32])
                slabs[n][core, y, x, z, 32 * at:32 * at + 16] = half.astype(BF16)
        if n < 2:
            for by in (4, 3, 5, 2, 6, 1, 7):
                push(n, 0, ("first",), own[n], device(moved("z", by), core))
        else:
            for step in (10, 2, 8, 6, 9, 11, 14, 1, 3, 4, 12, 5, 7, 13, 15):
                push(n, 0, ("first",), own[n], plane_peer(step))
    firsts = [slabs[0].at[core, y, x, pl.ds(0, 7)], slabs[1].at[core, y, x, pl.ds(0, 7)],
              slabs[2].at[core, pl.ds(0, 3), 0, pl.ds(0, 5)]]
    sent_views = []
    for n in (0, 1):
        sent_views += [firsts[n], slabs[n].at[0], slabs[n].at[:, :, pl.ds(0, 3), pl.ds(0, 5)]]
    sent_views += [firsts[2], slabs[2].at[0, :, :, pl.ds(0, 7)], slabs[2].at[0]]

    sq_group.wait_recv()
    total_sq = sq_buf[0]
    for step in range(1, 16):
        total_sq = total_sq + sq_buf[step]
    r_buf[tok] = lax.rsqrt(total_sq / D + EPS)
    start_all(r_copy)

    gain_copy.wait()

    def spread_gain(row, carry):
        wide = jnp.broadcast_to(gain_in[pl.ds(row, 1), :], (128, 128)).T
        index = row // 2
        y = (index // 16) * 2 + index % 2
        start = pl.multiple_of((row % 2) * 4, 4)
        gcol[(index // 2) % 2, y, (index // 4) % 4, pl.ds(start, 4)] = wide.reshape(4, 32, 128)
        return carry

    lax.fori_loop(0, 64, spread_gain, 0)

    def zero(block, carry):
        acc[pl.ds(pl.multiple_of(block * 64, 64), 64), :] = jnp.zeros((64, 512), F32)
        return carry

    lax.fori_loop(0, cap // 64, zero, 0)

    def piece(n, which, c_at, b_at):
        if n == 0:
            return slabs[0].at[which, b_at, c_at]
        return slabs[1].at[which, c_at, b_at]

    def plane(n, which, c_at):
        if n == 0:
            return slabs[0].at[which, :, c_at]
        if n == 1:
            return slabs[1].at[which, c_at]
        return slabs[2].at[which, :, :, c_at]

    def zhalf(c_at, half):
        return slabs[2].at[core, pl.ds(2 * half, 2), :, c_at]

    second = ("y", "x")

    def two_lines(n):
        return slabs[0].at[core, pl.ds(0, 2), x] if n == 0 else slabs[1].at[core, y, pl.ds(0, 2)]

    def two_planes(n, which):
        if n == 0:
            return slabs[0].at[which, :, pl.ds(0, 2)]
        if n == 1:
            return slabs[1].at[which, pl.ds(0, 2)]
        return slabs[2].at[which, :, :, pl.ds(0, 2)]

    def both_ways(n, name, b_at):
        axis = lasts[n]
        for side in (1, -1):
            push(n, 1, (name,), piece(n, core, here[axis], b_at), device(moved(axis, side), core))

    def go_on(n, name, b_at):
        axis = lasts[n]
        arrive(n, (name,), two_lines(n))
        push(n, 2, (name, "on"), piece(n, core, moved(axis, -way)[axis], b_at), device(moved(axis, way), core))

    def term_of(n, which, pick):
        weight = gcol[(which, *pick)].reshape(-1, 128)
        depth = weight.shape[0]
        lefts = []
        for at, (start, wide) in enumerate(blocks[n]):
            base = start // 128 * 128
            factor = r_rows[0:1, base:base + 128]
            if wide == 128:
                left = slabs[n][(which, *pick, slice(32 * at, 32 * at + 32))].astype(F32).reshape(depth, 128)
            else:
                left = slabs[n][(which, *pick, slice(32 * at, 32 * at + 16))].astype(F32).reshape(depth // 32, 16, 128)
                left = jnp.concatenate([left, pltpu.roll(left, 64, 2)], axis=1).reshape(depth, 128)
                if start != base:
                    factor = pltpu.roll(factor, 64, 1)
            lefts.append((left * factor * weight).astype(BF16)[:, :wide])
        left = jnp.concatenate(lefts, axis=1) if len(lefts) > 1 else lefts[0]
        right = w_all[(which, *pick)].reshape(depth, 512)
        return lax.dot_general(left, right, (((0,), (0,)), ((), ())), preferred_element_type=F32)

    def multiply(n, which, *picks):
        term = term_of(n, which, picks[0])
        for pick in picks[1:]:
            term = term + term_of(n, which, pick)
        row = 0
        for start, wide in blocks[n]:
            acc[start:start + wide, :] += term[row:row + wide]
            row += wide

    def shift(axis, by):
        return lax.rem(here[axis] + by, RING[axis])

    def each(count, work):
        def body(index, carry):
            work(index)
            return carry
        lax.fori_loop(0, count, body, 0)

    def both_cores(index):
        return lax.rem(core + index, 2)

    def whole(n, which, by):
        at = shift(lasts[n], by)
        multiply(n, which, (VALL, at, VALL) if n == 0 else (at, VALL, VALL))

    def some(n, which, by, steps):
        at = shift(lasts[n], by)
        places = [shift(second[n], step) for step in steps]
        multiply(n, which, *[(place, at, VALL) if n == 0 else (at, place, VALL) for place in places])

    def planes(count, first):
        each(2 * count, lambda index: multiply(
            2, both_cores(index // count), (VALL, VALL, shift("z", first + index % count))))

    def to_mate(n, sent, key, refs):
        for ref in refs:
            push(n, sent, ("mate", *key), ref, mate)

    def from_mate(n, key, view):
        arrive(n, ("mate", *key), view)

    for n in (0, 1):
        arrive(n, ("first",), firsts[n])
        axis = second[n]
        for side in (1, -1):
            push(n, 2, ("line",), piece(n, core, here[lasts[n]], here[axis]), device(moved(axis, side), core))
    for n in (0, 1):
        both_ways(n, "own", here[second[n]])
    arrive(2, ("first",), firsts[2])
    for half in (0, 1):
        for side in (1, -1):
            push(2, 1, ("wave", 0, half), zhalf(z, half), device(moved("z", side), core))
    to_mate(2, 2, (0,), [plane(2, core, z)])

    r_group.wait_recv()
    factors = [jnp.where(lane < 64, r_buf[2 * pair], r_buf[2 * pair + 1]) for pair in range(8)]
    factors = jnp.concatenate(factors, axis=1)
    factors = jnp.broadcast_to(factors, (16, 1024))
    digit_row = lax.broadcasted_iota(jnp.int32, (16, 1024), 0)
    table = jnp.zeros((16, 1024), F32)
    for digit, value in enumerate(split3(factors)):
        table = jnp.where(digit_row == digit, value, table)
    table = lax.dot_general(table.astype(BF16), onehot[...], (((1,), (1,)), ((), ())), preferred_element_type=F32)
    r_rows[...] = jnp.broadcast_to(table[0:1] + table[1:2] + table[2:3], r_rows.shape)

    pltpu.make_async_copy(w_all, w_all, local_sem.at[4]).wait()

    def zstep(step):
        for half in (0, 1):
            arrive(2, ("wave", step, half), slabs[2].at[core, pl.ds(0, 2), :, pl.ds(0, 2)])
            for side in (1, -1):
                at = moved("z", -side * (step + 1))["z"]
                if step < 2:
                    push(2, 1, ("wave", step + 1, half), zhalf(at, half), device(moved("z", side), core))
            if step == 2:
                push(2, 1, ("wave", 3, half), zhalf(moved("z", -way * 3)["z"], half), device(moved("z", way), core))
        sides = (step + 1, -step - 1)
        to_mate(2, 2, (step + 1,), [plane(2, core, moved("z", by)["z"]) for by in sides])

    ids_copy.wait()
    local_id = ids_in[...] - (tok * 16 + voc) * 512
    local_id = jnp.where((local_id >= 0) & (local_id < 512), local_id, 512)
    digits = jnp.where(lax.broadcasted_iota(jnp.int32, (16, 1024), 0) == 0, local_id // 256, local_id % 256)
    digits = digits.astype(F32).astype(BF16)
    cols = lax.dot_general(onehot[...], digits, (((1,), (1,)), ((), ())), preferred_element_type=F32)
    id_cols[...] = cols[:, 0:1] * 256.0 + cols[:, 1:2]
    student_copy.wait()
    st_rows[...] = jnp.dot(onehot[...], st_all[...], preferred_element_type=F32).astype(BF16)

    for n in (0, 1):
        axis = second[n]
        arrive(n, ("line",), two_lines(n))
        push(n, 2, ("opposite",), piece(n, core, here[lasts[n]], moved(axis, -way)[axis]), device(moved(axis, way), core))
    for n in (0, 1):
        axis = second[n]
        both_ways(n, "left", moved(axis, -1)[axis])
        both_ways(n, "right", moved(axis, 1)[axis])
    zstep(0)
    for n in (0, 1):
        go_on(n, "own", here[second[n]])
    for n in (0, 1):
        axis = second[n]
        arrive(n, ("opposite",), piece(n, core, here[lasts[n]], 0))
        both_ways(n, "far", moved(axis, 2)[axis])
    for n in (0, 1):
        to_mate(n, 2, (0,), [plane(n, core, here[lasts[n]])])
    zstep(1)

    def opposite(n, name, by):
        axis = second[n]
        b_at = moved(axis, by)[axis]
        arrive(n, (name, "on"), piece(n, core, here[lasts[n]], 0))
        c_at = moved(lasts[n], 2)[lasts[n]]
        to_mate(n, 2, ("far",) if name == "far" else ("early",), [piece(n, core, c_at, b_at)])

    for n in (0, 1):
        from_mate(n, (0,), plane(n, 1 - core, here[lasts[n]]))
        each(2, lambda index: whole(n, both_cores(index), 0))
    for n in (0, 1):
        go_on(n, "left", moved(second[n], -1)[second[n]])
    for n in (0, 1):
        go_on(n, "right", moved(second[n], 1)[second[n]])
    for n in (0, 1):
        opposite(n, "own", 0)
    zstep(2)
    from_mate(2, (0,), plane(2, 1 - core, z))
    from_mate(2, (1,), two_planes(2, 1 - core))
    from_mate(2, (2,), two_planes(2, 1 - core))
    planes(5, 6)
    for n in (0, 1):
        go_on(n, "far", moved(second[n], 2)[second[n]])
    for n in (0, 1):
        to_mate(n, 1, (1,), [plane(n, core, moved(lasts[n], side)[lasts[n]]) for side in (1, -1)])
    each(2, lambda index: whole(0, core, 1 + 2 * index))
    for n in (0, 1):
        opposite(n, "left", -1)
    for n in (0, 1):
        opposite(n, "right", 1)
    each(2, lambda index: whole(1, core, 1 + 2 * index))
    for half in (0, 1):
        arrive(2, ("wave", 3, half), zhalf(z, 0))
    at = moved("z", 4)["z"]
    to_mate(2, 2, (4,), [plane(2, core, at)])
    from_mate(0, (1,), two_planes(0, 1 - core))
    each(2, lambda index: whole(0, 1 - core, 1 + 2 * index))
    for n in (0, 1):
        opposite(n, "far", 2)
    from_mate(1, (1,), two_planes(1, 1 - core))
    each(2, lambda index: whole(1, 1 - core, 1 + 2 * index))
    from_mate(2, (3,), two_planes(2, 1 - core))
    from_mate(2, (4,), plane(2, 1 - core, at))
    planes(3, 3)
    for n in (0, 1):
        three = slabs[0].at[core, pl.ds(0, 3), x] if n == 0 else slabs[1].at[core, y, pl.ds(0, 3)]
        from_mate(n, ("early",), three)
        from_mate(n, ("far",), piece(n, 1 - core, here[lasts[n]], 0))
        each(2, lambda index: whole(n, both_cores(index), 2))

    lanes128 = lax.broadcasted_iota(jnp.int32, (64, 128), 1)
    lanes512 = lax.broadcasted_iota(jnp.int32, (64, 512), 1).astype(F32)

    def partials(start):
        take = pl.ds(start, 64)
        logits = acc[take, :]
        top = jnp.max(logits, axis=1, keepdims=True)
        low = logits - top
        expo = jnp.exp(low)
        total = jnp.sum(expo, axis=1, keepdims=True)
        cross = jnp.sum(expo * (low - st_rows[take, :].astype(F32)), axis=1, keepdims=True)
        pick = jnp.sum(jnp.where(lanes512 == id_cols[take, :], logits, 0.0), axis=1, keepdims=True)
        table = jnp.zeros((64, 128), F32)
        for at, value in enumerate((top, total, cross, pick)):
            for digit, part in enumerate(split3(value)):
                table = jnp.where(lanes128 == 8 * digit + at, part, table)
        stats[take, :] = table.astype(BF16)

    assert len(numbers) == NMSG, len(numbers)
    def partials256(block, carry):
        for piece in range(4):
            partials(pl.multiple_of(block * 256 + piece * 64, 64))
        return carry

    lax.fori_loop(0, cap // 256, partials256, 0)
    if cap % 256:
        partials(cap - 128)
        partials(cap - 64)
    spread = lax.dot_general(stats[...], onehot[...], (((0,), (0,)), ((), ())), preferred_element_type=F32)
    spread = spread[0:8] + spread[8:16] + spread[16:24]
    for pair in range(8):
        rows4 = spread[:, 128 * pair:128 * (pair + 1)]
        turned4 = pltpu.roll(rows4, 64, 1)
        fin_out[2 * pair] = jnp.where(lane < 64, rows4[0:2], turned4[2:4])
        fin_out[2 * pair + 1] = jnp.where(lane < 64, turned4[0:2], rows4[2:4])
    start_all(fin_a_copy)
    fin_a[0] = fin_out[tok]
    for at, view in enumerate(sent_views):
        pltpu.make_async_remote_copy(
            src_ref=view, dst_ref=view, send_sem=send_sem.at[at], recv_sem=recv_sem.at[0], device_id=mate,
            device_id_type=MESH).wait_send()
    for copies in (sq_group, a2a_group, r_group):
        copies.wait_send()
    fin_a_group.wait_recv()

    def combine(ref):
        every = ref[...]
        top, total = every[:, 0:1, :], every[:, 1:2, :]
        cross, pick = pltpu.roll(top, 64, 2), pltpu.roll(total, 64, 2)
        most = jnp.max(top, axis=0, keepdims=True)
        gap = top - most
        scale = jnp.exp(gap)
        return (most[0], jnp.sum(scale * total, axis=0), jnp.sum(scale * (cross + gap * total), axis=0),
                jnp.sum(pick, axis=0))

    sub = lax.broadcasted_iota(jnp.int32, (8, 128), 0)

    def table_of(values):
        table = jnp.zeros((8, 128), F32)
        for at, value in enumerate(values):
            table = jnp.where(sub == at, value, table)
        return table

    top, total, cross, pick = combine(fin_a)
    fin_b[0] = jnp.concatenate(
        [jnp.where(lane < 64, top, pltpu.roll(cross, 64, 1)), jnp.where(lane < 64, total, pltpu.roll(pick, 64, 1))], axis=0)
    start_all(fin_b_copy)
    fin_b_group.wait_recv()
    top, total, cross, pick = combine(fin_b)
    log_total = jnp.log(total)
    kl = cross / total - log_total
    logprob = pick - (top + log_total)
    valid = lane < lens[tok]
    out[...] = table_of((jnp.where(valid, kl, 0.0), jnp.where(valid, logprob, 0.0)))
    fin_a_group.wait_send()
    fin_b_group.wait_send()


def run(groups, number, hidden, gain, lengths, ids, student, head):
    cap = (sum(groups) + 1) // 2 * 128
    hbm = pl.BlockSpec(memory_space=pl.ANY)
    return pl.pallas_call(
        functools.partial(kernel, groups),
        out_shape=jax.ShapeDtypeStruct((8, 128), F32),
        in_specs=[hbm, hbm, pl.BlockSpec(memory_space=pltpu.SMEM), hbm, hbm, hbm],
        out_specs=pl.BlockSpec(memory_space=pltpu.VMEM),
        scratch_shapes=[pltpu.VMEM((2, 4, 4, 8, 16 * count, 128), BF16) for count in groups] + [
            pltpu.VMEM((2, 4, 4, 8, 32, 512), BF16),
            pltpu.VMEM((1024, 512), BF16),
            pltpu.VMEM((64, 512), BF16),
            pltpu.VMEM((64, 128), F32),
            pltpu.VMEM((1, 1024), jnp.int32),
            pltpu.VMEM((cap, 1024), BF16),
            pltpu.VMEM((cap, 512), BF16),
            pltpu.VMEM((cap, 1), F32),
            pltpu.VMEM((cap, 512), F32),
            pltpu.VMEM((cap, 128), BF16),
            pltpu.VMEM((2, 4, 4, 8, 32, 128), F32),
            pltpu.VMEM((8, cap), F32),
            pltpu.VMEM((16, 1, 128), F32),
            pltpu.VMEM((16, 1, 128), F32),
            pltpu.VMEM((16, 16, 128), BF16),
            pltpu.VMEM((16, 16, 128), BF16),
            pltpu.VMEM((16, 2, 128), F32),
            pltpu.VMEM((16, 2, 128), F32),
            pltpu.VMEM((16, 2, 128), F32),
            pltpu.SemaphoreType.DMA((5,)),
            pltpu.SemaphoreType.DMA((10,)),
            pltpu.SemaphoreType.DMA((9,)),
            pltpu.SemaphoreType.DMA((NMSG,)),
        ],
        compiler_params=pltpu.CompilerParams(
            collective_id=number, has_side_effects=True, vmem_limit_bytes=60 * 1024 * 1024),
        name="gathered_head_%d" % (64 * sum(groups)),
    )(hidden, gain, lengths, ids, student, head)


SPLITS = ((3, 3, 2), (3, 3, 3), (4, 4, 2), (6, 6, 4))


def per_device(hidden, gain, head_weight, student, token_ids, lengths):
    args = (hidden, gain.reshape(64, 128), lengths, token_ids.reshape(1, -1), student,
            head_weight.reshape(32, 8, 32, head_weight.shape[1]))
    if len(SPLITS) == 1:
        table = run(SPLITS[0], 0, *args)
    else:
        tokens = jnp.sum(lengths)
        which = sum((tokens > 64 * sum(groups)).astype(jnp.int32) for groups in SPLITS[:-1])
        table = lax.switch(which, [functools.partial(run, groups, at) for at, groups in enumerate(SPLITS)], *args)
    return table[0, :64], table[1, :64]


def solution(mesh):
    placed = (P("tok", "voc"), P(), P(None, ("tok", "voc")), P(None, ("tok", "voc")), P(), P())
    return jax.shard_map(
        per_device, mesh=mesh, in_specs=placed, out_specs=(P("tok"), P("tok")), check_vma=False
    )
```

```python
import functools

import jax
import jax.numpy as jnp
from jax import lax
from jax.experimental import pallas as pl
from jax.experimental.pallas import tpu as pltpu
from jax.sharding import PartitionSpec as P

D = 8192
LEN = 64
EPS = 1e-06
MESH = pl.DeviceIdType.MESH
F32 = jnp.float32
BF16 = jnp.bfloat16
RING = {"y": 4, "x": 4, "z": 8}
VALL = slice(None)


def split3(value):
    hi = value.astype(BF16).astype(F32)
    rest = value - hi
    mid = rest.astype(BF16).astype(F32)
    return hi, mid, (rest - mid).astype(BF16).astype(F32)


def blocks_of(groups):
    blocks = [[] for _ in groups]
    start = 0
    for part, count in enumerate(groups):
        for _ in range(count // 2):
            blocks[part].append((start, 0, 32))
            start += 128
    if groups[0] % 2:
        blocks[0].append((start, 0, 16))
        blocks[1].append((start, 16, 16))
    return blocks


def kernel(groups, hidden, gain, lens, ids, student, head, out, *scratch):
    cap = (sum(groups) + 1) // 2 * 128
    blocks = blocks_of(groups)
    lasts = ("x", "y", "z")
    has_z = groups[2] > 0
    slabs = scratch[:3]
    (w_all, st_all, h_in, gain_in, ids_in, onehot, st_rows, id_cols, acc, stats, gcol, r_rows, sq_buf, r_buf, a2a_out,
     a2a_in, fin_out, fin_a, fin_b, local_sem, pair_sem, send_sem, recv_sem) = scratch[3:]
    tok = lax.axis_index("tok")
    voc = lax.axis_index("voc")
    here = {"y": (voc // 8) * 2 + tok // 8, "x": (voc // 2) % 4, "z": tok % 8}
    core = voc % 2
    way = 1 - 2 * core

    def device(place, which):
        return {"tok": (place["y"] % 2) * 8 + place["z"], "voc": ((place["y"] // 2) * 4 + place["x"]) * 2 + which}

    def moved(axis, by):
        place = dict(here)
        place[axis] = lax.rem(here[axis] + by + RING[axis], RING[axis])
        return place

    def tok_peer(step):
        return {"tok": lax.rem(tok + step, 16), "voc": voc}

    def voc_peer(step):
        return {"tok": tok, "voc": lax.rem(voc + step, 16)}

    def plane_peer(step):
        return device({"y": lax.rem(here["y"] + step // 4, 4), "x": lax.rem(here["x"] + step % 4, 4), "z": here["z"]}, core)

    hidden_copy = pltpu.make_async_copy(hidden, h_in, local_sem.at[0])
    hidden_copy.start()
    barrier = pltpu.get_barrier_semaphore()

    def greet(step, carry):
        pl.semaphore_signal(barrier, inc=1, device_id=tok_peer(step), device_id_type=MESH)
        pl.semaphore_signal(barrier, inc=1, device_id=voc_peer(step), device_id_type=MESH)
        return carry

    lax.fori_loop(1, 16, greet, 0)
    for step in range(4, 16):
        dy, dx = step // 4, step % 4
        if dy % 2 and dx and has_z:
            pl.semaphore_signal(barrier, inc=1, device_id=plane_peer(step), device_id_type=MESH)
    across = {"tok": lax.rem(tok + 8, 16), "voc": lax.rem(voc + 8, 16)}
    pl.semaphore_signal(barrier, inc=1, device_id=across, device_id_type=MESH)

    def head_copy(index):
        y = (index // 16) * 2 + index % 2
        return pltpu.make_async_copy(
            head.at[index], w_all.at[(index // 2) % 2, y, (index // 4) % 4], local_sem.at[4]
        )

    gain_copy = pltpu.make_async_copy(gain, gain_in, local_sem.at[1])
    ids_copy = pltpu.make_async_copy(ids, ids_in, local_sem.at[2])
    student_copy = pltpu.make_async_copy(student, st_all, local_sem.at[3])
    hidden_copy.wait()
    rows = h_in[...].astype(F32)
    rows = jnp.concatenate([rows, rows], axis=0)
    turned = rows.T
    square = jnp.sum(turned * turned, axis=0, keepdims=True)
    sq_buf[0] = square
    lane = lax.broadcasted_iota(jnp.int32, (1, 128), 1)
    turned = turned.reshape(16, 32, 128)
    a2a_out[...] = jnp.where(lane[None] < 64, turned[:, 0:16], turned[:, 16:32]).astype(BF16)

    pl.semaphore_wait(barrier, 37 if has_z else 31)

    def sq_copy(step):
        return pltpu.make_async_remote_copy(
            src_ref=sq_buf.at[0], dst_ref=sq_buf.at[step], send_sem=pair_sem.at[0],
            recv_sem=pair_sem.at[1], device_id=voc_peer(step), device_id_type=MESH)

    def a2a_copy(step):
        return pltpu.make_async_remote_copy(
            src_ref=a2a_out.at[lax.rem(tok + step, 16)], dst_ref=a2a_in.at[tok], send_sem=pair_sem.at[2],
            recv_sem=pair_sem.at[3], device_id=tok_peer(step), device_id_type=MESH)

    def r_copy(step):
        return pltpu.make_async_remote_copy(
            src_ref=r_buf.at[tok], dst_ref=r_buf.at[tok], send_sem=pair_sem.at[8],
            recv_sem=pair_sem.at[9], device_id=tok_peer(step), device_id_type=MESH)

    def fin_a_copy(step):
        return pltpu.make_async_remote_copy(
            src_ref=fin_out.at[lax.rem(tok + step, 16)], dst_ref=fin_a.at[step], send_sem=pair_sem.at[4],
            recv_sem=pair_sem.at[5], device_id=tok_peer(step), device_id_type=MESH)

    def fin_b_copy(step):
        return pltpu.make_async_remote_copy(
            src_ref=fin_b.at[0], dst_ref=fin_b.at[step], send_sem=pair_sem.at[6],
            recv_sem=pair_sem.at[7], device_id=voc_peer(step), device_id_type=MESH)

    def start_all(copy):
        def body(step, carry):
            copy(step).start()
            return carry
        lax.fori_loop(1, 16, body, 0)

    def group(ref, first, at):
        view = ref.at[pl.ds(first, 15)]
        return pltpu.make_async_remote_copy(
            src_ref=view, dst_ref=view, send_sem=pair_sem.at[at], recv_sem=pair_sem.at[at + 1],
            device_id=tok_peer(1), device_id_type=MESH)

    sq_group, a2a_group, r_group = group(sq_buf, 1, 0), group(a2a_in, 0, 2), group(r_buf, 0, 8)
    fin_a_group, fin_b_group = group(fin_a, 1, 4), group(fin_b, 1, 6)

    start_all(a2a_copy)
    start_all(sq_copy)
    a2a_in[tok] = a2a_out[tok]

    gain_copy.start()
    ids_copy.start()
    student_copy.start()

    def load(index, carry):
        head_copy(index).start()
        return carry

    lax.fori_loop(0, 32, load, 0)

    place_of = []
    offset = jnp.int32(0)
    for pair in range(8):
        first, second = lens[2 * pair], lens[2 * pair + 1]
        low = jnp.where(lane < first, offset + lane, -1)
        high = jnp.where(lane - 64 < second, offset + first + lane - 64, -1)
        place_of.append(jnp.where(lane < 64, low, high))
        offset = offset + first + second
    place_of = jnp.concatenate(place_of, axis=1)

    def fill(block, carry):
        start = pl.multiple_of(block * 64, 64)
        want = lax.broadcasted_iota(jnp.int32, (64, 1024), 0) + start
        onehot[pl.ds(start, 64), :] = jnp.where(want == place_of, 1.0, 0.0).astype(BF16)
        return carry

    lax.fori_loop(0, cap // 64, fill, 0)


    gain_copy.wait()

    def spread_gain(row, carry):
        wide = jnp.broadcast_to(gain_in[pl.ds(row, 1), :], (128, 128)).T
        index = row // 2
        y = (index // 16) * 2 + index % 2
        start = pl.multiple_of((row % 2) * 4, 4)
        gcol[(index // 2) % 2, y, (index // 4) % 4, pl.ds(start, 4)] = wide.reshape(4, 32, 128)
        return carry

    lax.fori_loop(0, 32, spread_gain, 0, unroll=2)
    a2a_group.wait_recv()
    pieces = []
    for pair in range(8):
        low, high = a2a_in[2 * pair].astype(F32), a2a_in[2 * pair + 1].astype(F32)
        upper = jnp.where(lane < 64, low, pltpu.roll(high, 64, 1))
        under = jnp.where(lane < 64, pltpu.roll(low, 64, 1), high)
        pieces.append(jnp.concatenate([upper, under], axis=0))
    block = jnp.concatenate(pieces, axis=1).astype(BF16)
    packed = lax.dot_general(block, onehot[...], (((1,), (1,)), ((), ())), preferred_element_type=F32)

    numbers = {}

    def number_of(*key):
        return numbers.setdefault(key, len(numbers))

    def push(n, sent, key, src, target):
        if n == 2 and not has_z:
            return
        pltpu.make_async_remote_copy(
            src_ref=src, dst_ref=src, send_sem=send_sem.at[3 * n + sent], recv_sem=recv_sem.at[number_of(n, *key)],
            device_id=target, device_id_type=MESH).start()

    def arrive(n, key, view):
        if n == 2 and not has_z:
            return
        pltpu.make_async_remote_copy(
            src_ref=view, dst_ref=view, send_sem=send_sem.at[0], recv_sem=recv_sem.at[number_of(n, *key)],
            device_id=mate, device_id_type=MESH).wait_recv()

    mate = device(here, 1 - core)
    y, x, z = here["y"], here["x"], here["z"]
    own = [slab.at[core, y, x, z] for slab in slabs]
    for n in range(3):
        for at, (start, row, rows) in enumerate(blocks[n]):
            slabs[n][core, y, x, z, 32 * at:32 * at + rows] = packed[row:row + rows, start:start + 128].astype(BF16)
        if n < 2:
            for by in (4, 3, 5, 2, 6, 1, 7):
                push(n, 0, ("first",), own[n], device(moved("z", by), core))
        elif has_z:
            for step in (10, 2, 8, 6, 9, 11, 14, 1, 3, 4, 12, 5, 7, 13, 15):
                push(n, 0, ("first",), own[n], plane_peer(step))
    firsts = [slabs[0].at[core, y, x, pl.ds(0, 7)], slabs[1].at[core, y, x, pl.ds(0, 7)],
              slabs[2].at[core, pl.ds(0, 3), 0, pl.ds(0, 5)]]
    sent_views = []
    for n in (0, 1):
        sent_views += [firsts[n], slabs[n].at[0], slabs[n].at[:, :, pl.ds(0, 3), pl.ds(0, 5)]]
    if has_z:
        sent_views += [firsts[2], slabs[2].at[0, :, :, pl.ds(0, 7)], slabs[2].at[0]]

    sq_group.wait_recv()
    total_sq = sq_buf[0]
    for step in range(1, 16):
        total_sq = total_sq + sq_buf[step]
    r_buf[tok] = lax.rsqrt(total_sq / D + EPS)
    start_all(r_copy)

    lax.fori_loop(32, 64, spread_gain, 0, unroll=2)

    def zero(block, carry):
        acc[pl.ds(pl.multiple_of(block * 64, 64), 64), :] = jnp.zeros((64, 512), F32)
        return carry

    lax.fori_loop(0, cap // 64, zero, 0)

    def piece(n, which, c_at, b_at):
        if n == 0:
            return slabs[0].at[which, b_at, c_at]
        return slabs[1].at[which, c_at, b_at]

    def plane(n, which, c_at):
        if n == 0:
            return slabs[0].at[which, :, c_at]
        if n == 1:
            return slabs[1].at[which, c_at]
        return slabs[2].at[which, :, :, c_at]

    def zhalf(c_at, half):
        return slabs[2].at[core, pl.ds(2 * half, 2), :, c_at]

    second = ("y", "x")

    def two_lines(n):
        return slabs[0].at[core, pl.ds(0, 2), x] if n == 0 else slabs[1].at[core, y, pl.ds(0, 2)]

    def two_planes(n, which):
        if n == 0:
            return slabs[0].at[which, :, pl.ds(0, 2)]
        if n == 1:
            return slabs[1].at[which, pl.ds(0, 2)]
        return slabs[2].at[which, :, :, pl.ds(0, 2)]

    def both_ways(n, name, b_at):
        axis = lasts[n]
        for side in (1, -1):
            push(n, 1, (name,), piece(n, core, here[axis], b_at), device(moved(axis, side), core))

    def go_on(n, name, b_at):
        axis = lasts[n]
        arrive(n, (name,), two_lines(n))
        push(n, 2, (name, "on"), piece(n, core, moved(axis, -way)[axis], b_at), device(moved(axis, way), core))

    def multiply(n, which, pick):
        if n == 2 and not has_z:
            return
        for row, rows in ((0, 32), (0, 16), (16, 16)):
            chosen = [(at, block[0]) for at, block in enumerate(blocks[n]) if block[1:] == (row, rows)]
            if not chosen:
                continue
            take = (which, *pick, slice(row, row + rows))
            weight = gcol[take].reshape(-1, 128)
            depth = weight.shape[0]
            lefts = []
            for at, start in chosen:
                left = slabs[n][(which, *pick, slice(32 * at, 32 * at + rows))].astype(F32).reshape(depth, 128)
                lefts.append((left * r_rows[0:1, start:start + 128] * weight).astype(BF16))
            left = jnp.concatenate(lefts, axis=1) if len(lefts) > 1 else lefts[0]
            right = w_all[take].reshape(depth, 512)
            term = lax.dot_general(left, right, (((0,), (0,)), ((), ())), preferred_element_type=F32)
            first = chosen[0][1]
            acc[first:first + 128 * len(chosen), :] += term

    def shift(axis, by):
        return lax.rem(here[axis] + by, RING[axis])

    def each(count, work, wanted=True):
        if not wanted:
            return
        def body(index, carry):
            work(index)
            return carry
        lax.fori_loop(0, count, body, 0)

    def both_cores(index):
        return lax.rem(core + index, 2)

    def whole(n, which, by):
        at = shift(lasts[n], by)
        multiply(n, which, (VALL, at, VALL) if n == 0 else (at, VALL, VALL))

    def planes(which, count, first, stride=1):
        each(count, lambda index: multiply(2, which, (VALL, VALL, shift("z", first + stride * index))), has_z)

    def to_mate(n, sent, key, refs):
        for ref in refs:
            push(n, sent, ("mate", *key), ref, mate)

    def from_mate(n, key, view):
        arrive(n, ("mate", *key), view)

    for n in (0, 1):
        arrive(n, ("first",), firsts[n])
        axis = second[n]
        for side in (1, -1):
            push(n, 2, ("line",), piece(n, core, here[lasts[n]], here[axis]), device(moved(axis, side), core))
    for n in (0, 1):
        both_ways(n, "own", here[second[n]])
    arrive(2, ("first",), firsts[2])
    for half in (0, 1) if has_z else ():
        for side in (1, -1):
            push(2, 1, ("wave", 0, half), zhalf(z, half), device(moved("z", side), core))
    to_mate(2, 2, (0,), [plane(2, core, z)])

    r_group.wait_recv()
    factors = [jnp.where(lane < 64, r_buf[2 * pair], r_buf[2 * pair + 1]) for pair in range(8)]
    factors = jnp.concatenate(factors, axis=1)
    factors = jnp.broadcast_to(factors, (16, 1024))
    digit_row = lax.broadcasted_iota(jnp.int32, (16, 1024), 0)
    table = jnp.zeros((16, 1024), F32)
    for digit, value in enumerate(split3(factors)):
        table = jnp.where(digit_row == digit, value, table)
    table = lax.dot_general(table.astype(BF16), onehot[...], (((1,), (1,)), ((), ())), preferred_element_type=F32)
    r_rows[...] = jnp.broadcast_to(table[0:1] + table[1:2] + table[2:3], r_rows.shape)

    pltpu.make_async_copy(w_all, w_all, local_sem.at[4]).wait()

    def zstep(step):
        for half in (0, 1):
            arrive(2, ("wave", step, half), slabs[2].at[core, pl.ds(0, 2), :, pl.ds(0, 2)])
            for side in (1, -1):
                at = moved("z", -side * (step + 1))["z"]
                if step < 2:
                    push(2, 1, ("wave", step + 1, half), zhalf(at, half), device(moved("z", side), core))
            if step == 2:
                push(2, 1, ("wave", 3, half), zhalf(moved("z", -way * 3)["z"], half), device(moved("z", way), core))
        sides = (step + 1, -step - 1)
        to_mate(2, 2, (step + 1,), [plane(2, core, moved("z", by)["z"]) for by in sides])

    ids_copy.wait()
    local_id = ids_in[...] - (tok * 16 + voc) * 512
    local_id = jnp.where((local_id >= 0) & (local_id < 512), local_id, 512)
    digits = jnp.where(lax.broadcasted_iota(jnp.int32, (16, 1024), 0) == 0, local_id // 256, local_id % 256)
    digits = digits.astype(F32).astype(BF16)
    cols = lax.dot_general(onehot[...], digits, (((1,), (1,)), ((), ())), preferred_element_type=F32)
    id_cols[...] = cols[:, 0:1] * 256.0 + cols[:, 1:2]
    student_copy.wait()
    st_rows[...] = jnp.dot(onehot[...], st_all[...], preferred_element_type=F32).astype(BF16)

    for n in (0, 1):
        axis = second[n]
        arrive(n, ("line",), two_lines(n))
        push(n, 2, ("opposite",), piece(n, core, here[lasts[n]], moved(axis, -way)[axis]), device(moved(axis, way), core))
    for n in (0, 1):
        axis = second[n]
        both_ways(n, "left", moved(axis, -1)[axis])
        both_ways(n, "right", moved(axis, 1)[axis])
    zstep(0)
    planes(core, 3, 7)
    for n in (0, 1):
        go_on(n, "own", here[second[n]])
    for n in (0, 1):
        axis = second[n]
        arrive(n, ("opposite",), piece(n, core, here[lasts[n]], 0))
        both_ways(n, "far", moved(axis, 2)[axis])
    for n in (0, 1):
        to_mate(n, 2, (0,), [plane(n, core, here[lasts[n]])])
    from_mate(2, (0,), plane(2, 1 - core, z))
    from_mate(2, (1,), two_planes(2, 1 - core))
    planes(1 - core, 3, 7)
    zstep(1)

    def opposite(n, name, by):
        axis = second[n]
        b_at = moved(axis, by)[axis]
        arrive(n, (name, "on"), piece(n, core, here[lasts[n]], 0))
        c_at = moved(lasts[n], 2)[lasts[n]]
        to_mate(n, 2, ("far",) if name == "far" else ("early",), [piece(n, core, c_at, b_at)])

    for n in (0, 1):
        from_mate(n, (0,), plane(n, 1 - core, here[lasts[n]]))
        each(2, lambda index: whole(n, both_cores(index), 0))
    for n in (0, 1):
        go_on(n, "left", moved(second[n], -1)[second[n]])
    for n in (0, 1):
        go_on(n, "right", moved(second[n], 1)[second[n]])
    for n in (0, 1):
        opposite(n, "own", 0)
    planes(core, 2, 2, 4)
    zstep(2)
    from_mate(2, (2,), two_planes(2, 1 - core))
    planes(1 - core, 2, 2, 4)
    for n in (0, 1):
        go_on(n, "far", moved(second[n], 2)[second[n]])
    for n in (0, 1):
        to_mate(n, 1, (1,), [plane(n, core, moved(lasts[n], side)[lasts[n]]) for side in (1, -1)])
    each(2, lambda index: whole(0, core, 1 + 2 * index))
    planes(core, 2, 3, 2)
    for n in (0, 1):
        opposite(n, "left", -1)
    for n in (0, 1):
        opposite(n, "right", 1)
    each(2, lambda index: whole(1, core, 1 + 2 * index))
    for half in (0, 1):
        arrive(2, ("wave", 3, half), zhalf(z, 0))
    at = moved("z", 4)["z"]
    to_mate(2, 2, (4,), [plane(2, core, at)])
    from_mate(0, (1,), two_planes(0, 1 - core))
    each(2, lambda index: whole(0, 1 - core, 1 + 2 * index))
    for n in (0, 1):
        opposite(n, "far", 2)
    from_mate(1, (1,), two_planes(1, 1 - core))
    each(2, lambda index: whole(1, 1 - core, 1 + 2 * index))
    from_mate(2, (3,), two_planes(2, 1 - core))
    planes(1 - core, 2, 3, 2)
    from_mate(2, (4,), plane(2, 1 - core, at))
    each(2, lambda index: multiply(2, both_cores(index), (VALL, VALL, shift("z", 4))), has_z)
    for n in (0, 1):
        three = slabs[0].at[core, pl.ds(0, 3), x] if n == 0 else slabs[1].at[core, y, pl.ds(0, 3)]
        from_mate(n, ("early",), three)
        from_mate(n, ("far",), piece(n, 1 - core, here[lasts[n]], 0))
        each(2, lambda index: whole(n, both_cores(index), 2))

    lanes128 = lax.broadcasted_iota(jnp.int32, (64, 128), 1)
    lanes512 = lax.broadcasted_iota(jnp.int32, (64, 512), 1).astype(F32)

    def partials(start):
        take = pl.ds(start, 64)
        logits = acc[take, :]
        top = jnp.max(logits, axis=1, keepdims=True)
        low = logits - top
        expo = jnp.exp(low)
        total = jnp.sum(expo, axis=1, keepdims=True)
        cross = jnp.sum(expo * (low - st_rows[take, :].astype(F32)), axis=1, keepdims=True)
        pick = jnp.sum(jnp.where(lanes512 == id_cols[take, :], logits, 0.0), axis=1, keepdims=True)
        table = jnp.zeros((64, 128), F32)
        for at, value in enumerate((top, total, cross, pick)):
            for digit, part in enumerate(split3(value)):
                table = jnp.where(lanes128 == 8 * digit + at, part, table)
        stats[take, :] = table.astype(BF16)

    assert len(numbers) == (44 if has_z else 30)
    def partials256(block, carry):
        for piece in range(4):
            partials(pl.multiple_of(block * 256 + piece * 64, 64))
        return carry

    lax.fori_loop(0, cap // 256, partials256, 0)
    if cap % 256:
        partials(cap - 128)
        partials(cap - 64)
    spread = lax.dot_general(stats[...][:, 0:32], onehot[...], (((0,), (0,)), ((), ())), preferred_element_type=F32)
    spread = spread[0:8] + spread[8:16] + spread[16:24]
    for pair in range(8):
        rows4 = spread[:, 128 * pair:128 * (pair + 1)]
        turned4 = pltpu.roll(rows4, 64, 1)
        fin_out[2 * pair] = jnp.where(lane < 64, rows4[0:2], turned4[2:4])
        fin_out[2 * pair + 1] = jnp.where(lane < 64, turned4[0:2], rows4[2:4])
    start_all(fin_a_copy)
    fin_a[0] = fin_out[tok]
    for at, view in enumerate(sent_views):
        pltpu.make_async_remote_copy(
            src_ref=view, dst_ref=view, send_sem=send_sem.at[at], recv_sem=recv_sem.at[0], device_id=mate,
            device_id_type=MESH).wait_send()
    for copies in (sq_group, a2a_group, r_group):
        copies.wait_send()
    fin_a_group.wait_recv()

    def combine(ref):
        every = ref[...]
        top, total = every[:, 0:1, :], every[:, 1:2, :]
        cross, pick = pltpu.roll(top, 64, 2), pltpu.roll(total, 64, 2)
        most = jnp.max(top, axis=0, keepdims=True)
        gap = top - most
        scale = jnp.exp(gap)
        return (most[0], jnp.sum(scale * total, axis=0), jnp.sum(scale * (cross + gap * total), axis=0),
                jnp.sum(pick, axis=0))

    sub = lax.broadcasted_iota(jnp.int32, (8, 128), 0)

    def table_of(values):
        table = jnp.zeros((8, 128), F32)
        for at, value in enumerate(values):
            table = jnp.where(sub == at, value, table)
        return table

    top, total, cross, pick = combine(fin_a)
    fin_b[0] = jnp.concatenate(
        [jnp.where(lane < 64, top, pltpu.roll(cross, 64, 1)), jnp.where(lane < 64, total, pltpu.roll(pick, 64, 1))], axis=0)
    start_all(fin_b_copy)
    fin_b_group.wait_recv()
    top, total, cross, pick = combine(fin_b)
    log_total = jnp.log(total)
    kl = cross / total - log_total
    logprob = pick - (top + log_total)
    valid = lane < lens[tok]
    out[...] = table_of((jnp.where(valid, kl, 0.0), jnp.where(valid, logprob, 0.0)))
    fin_a_group.wait_send()
    fin_b_group.wait_send()


def run(groups, number, hidden, gain, lengths, ids, student, head):
    cap = (sum(groups) + 1) // 2 * 128
    hbm = pl.BlockSpec(memory_space=pl.ANY)
    return pl.pallas_call(
        functools.partial(kernel, groups),
        out_shape=jax.ShapeDtypeStruct((8, 128), F32),
        in_specs=[hbm, hbm, pl.BlockSpec(memory_space=pltpu.SMEM), hbm, hbm, hbm],
        out_specs=pl.BlockSpec(memory_space=pltpu.VMEM),
        scratch_shapes=[pltpu.VMEM((2, 4, 4, 8, 16 * max(count, 1), 128), BF16) for count in groups] + [
            pltpu.VMEM((2, 4, 4, 8, 32, 512), BF16),
            pltpu.VMEM((1024, 512), BF16),
            pltpu.VMEM((64, 512), BF16),
            pltpu.VMEM((64, 128), F32),
            pltpu.VMEM((1, 1024), jnp.int32),
            pltpu.VMEM((cap, 1024), BF16),
            pltpu.VMEM((cap, 512), BF16),
            pltpu.VMEM((cap, 1), F32),
            pltpu.VMEM((cap, 512), F32),
            pltpu.VMEM((cap, 128), BF16),
            pltpu.VMEM((2, 4, 4, 8, 32, 128), F32),
            pltpu.VMEM((8, cap), F32),
            pltpu.VMEM((16, 1, 128), F32),
            pltpu.VMEM((16, 1, 128), F32),
            pltpu.VMEM((16, 16, 128), BF16),
            pltpu.VMEM((16, 16, 128), BF16),
            pltpu.VMEM((16, 2, 128), F32),
            pltpu.VMEM((16, 2, 128), F32),
            pltpu.VMEM((16, 2, 128), F32),
            pltpu.SemaphoreType.DMA((5,)),
            pltpu.SemaphoreType.DMA((10,)),
            pltpu.SemaphoreType.DMA((9,)),
            pltpu.SemaphoreType.DMA((44 if groups[2] else 30,)),
        ],
        compiler_params=pltpu.CompilerParams(
            collective_id=number, has_side_effects=True, vmem_limit_bytes=60 * 1024 * 1024),
        name="gathered_head_%d" % (64 * sum(groups)),
    )(hidden, gain, lengths, ids, student, head)


SPLITS = ((3, 3, 2), (4, 4, 2), (6, 6, 4))


def per_device(hidden, gain, head_weight, student, token_ids, lengths):
    args = (hidden, gain.reshape(64, 128), lengths, token_ids.reshape(1, -1), student,
            head_weight.reshape(32, 8, 32, head_weight.shape[1]))
    if len(SPLITS) == 1:
        table = run(SPLITS[0], 0, *args)
    else:
        tokens = jnp.sum(lengths)
        which = sum((tokens > 64 * sum(groups)).astype(jnp.int32) for groups in SPLITS[:-1])
        table = lax.switch(which, [functools.partial(run, groups, at) for at, groups in enumerate(SPLITS)], *args)
    return table[0, :64], table[1, :64]


def solution(mesh):
    placed = (P("tok", "voc"), P(), P(None, ("tok", "voc")), P(None, ("tok", "voc")), P(), P())
    return jax.shard_map(
        per_device, mesh=mesh, in_specs=placed, out_specs=(P("tok"), P("tok")), check_vma=False
    )
```

```python
import functools

import jax
import jax.numpy as jnp
from jax import lax
from jax.experimental import pallas as pl
from jax.experimental.pallas import tpu as pltpu
from jax.sharding import PartitionSpec as P

D = 8192
LEN = 64
EPS = 1e-06
MESH = pl.DeviceIdType.MESH
F32 = jnp.float32
BF16 = jnp.bfloat16
RING = {"y": 4, "x": 4, "z": 8}
VALL = slice(None)


def split3(value):
    hi = value.astype(BF16).astype(F32)
    rest = value - hi
    mid = rest.astype(BF16).astype(F32)
    return hi, mid, (rest - mid).astype(BF16).astype(F32)


def blocks_of(groups):
    blocks = [[] for _ in groups]
    start = 0
    for part, count in enumerate(groups):
        for _ in range(count // 2):
            blocks[part].append((start, 0, 32))
            start += 128
    if groups[0] % 2:
        blocks[0].append((start, 0, 16))
        blocks[1].append((start, 16, 16))
    return blocks


def kernel(groups, hidden, gain, lens, ids, student, head, out, *scratch):
    cap = (sum(groups) + 1) // 2 * 128
    blocks = blocks_of(groups)
    lasts = ("x", "y", "z")
    has_z = groups[2] > 0
    slabs = scratch[:3]
    (w_all, st_all, h_in, gain_in, ids_in, onehot, st_rows, id_cols, acc, stats, gcol, r_rows, sq_buf, r_buf, a2a_out,
     a2a_in, fin_out, fin_a, fin_b, local_sem, pair_sem, send_sem, recv_sem) = scratch[3:]
    tok = lax.axis_index("tok")
    voc = lax.axis_index("voc")
    here = {"y": (voc // 8) * 2 + tok // 8, "x": (voc // 2) % 4, "z": tok % 8}
    core = voc % 2
    way = 1 - 2 * core

    def device(place, which):
        return {"tok": (place["y"] % 2) * 8 + place["z"], "voc": ((place["y"] // 2) * 4 + place["x"]) * 2 + which}

    def moved(axis, by):
        place = dict(here)
        place[axis] = lax.rem(here[axis] + by + RING[axis], RING[axis])
        return place

    def tok_peer(step):
        return {"tok": lax.rem(tok + step, 16), "voc": voc}

    def voc_peer(step):
        return {"tok": tok, "voc": lax.rem(voc + step, 16)}

    def plane_peer(step):
        return device({"y": lax.rem(here["y"] + step // 4, 4), "x": lax.rem(here["x"] + step % 4, 4), "z": here["z"]}, core)

    hidden_copy = pltpu.make_async_copy(hidden, h_in, local_sem.at[0])
    hidden_copy.start()
    barrier = pltpu.get_barrier_semaphore()

    def greet(step, carry):
        pl.semaphore_signal(barrier, inc=1, device_id=tok_peer(step), device_id_type=MESH)
        pl.semaphore_signal(barrier, inc=1, device_id=voc_peer(step), device_id_type=MESH)
        return carry

    lax.fori_loop(1, 16, greet, 0)
    for step in range(4, 16):
        dy, dx = step // 4, step % 4
        if dy % 2 and dx and has_z:
            pl.semaphore_signal(barrier, inc=1, device_id=plane_peer(step), device_id_type=MESH)
    across = {"tok": lax.rem(tok + 8, 16), "voc": lax.rem(voc + 8, 16)}
    pl.semaphore_signal(barrier, inc=1, device_id=across, device_id_type=MESH)

    def head_copy(index):
        y = (index // 16) * 2 + index % 2
        return pltpu.make_async_copy(
            head.at[index], w_all.at[(index // 2) % 2, y, (index // 4) % 4], local_sem.at[4]
        )

    gain_copy = pltpu.make_async_copy(gain, gain_in, local_sem.at[1])
    ids_copy = pltpu.make_async_copy(ids, ids_in, local_sem.at[2])
    student_copy = pltpu.make_async_copy(student, st_all, local_sem.at[3])
    hidden_copy.wait()
    rows = h_in[...].astype(F32)
    rows = jnp.concatenate([rows, rows], axis=0)
    turned = rows.T
    square = jnp.sum(turned * turned, axis=0, keepdims=True)
    sq_buf[0] = square
    lane = lax.broadcasted_iota(jnp.int32, (1, 128), 1)
    turned = turned.reshape(16, 32, 128)
    a2a_out[...] = jnp.where(lane[None] < 64, turned[:, 0:16], turned[:, 16:32]).astype(BF16)

    pl.semaphore_wait(barrier, 37 if has_z else 31)

    def sq_copy(step):
        return pltpu.make_async_remote_copy(
            src_ref=sq_buf.at[0], dst_ref=sq_buf.at[step], send_sem=pair_sem.at[0],
            recv_sem=pair_sem.at[1], device_id=voc_peer(step), device_id_type=MESH)

    def a2a_copy(step):
        return pltpu.make_async_remote_copy(
            src_ref=a2a_out.at[lax.rem(tok + step, 16)], dst_ref=a2a_in.at[tok], send_sem=pair_sem.at[2],
            recv_sem=pair_sem.at[3], device_id=tok_peer(step), device_id_type=MESH)

    def r_copy(step):
        return pltpu.make_async_remote_copy(
            src_ref=r_buf.at[tok], dst_ref=r_buf.at[tok], send_sem=pair_sem.at[8],
            recv_sem=pair_sem.at[9], device_id=tok_peer(step), device_id_type=MESH)

    def fin_a_copy(step):
        return pltpu.make_async_remote_copy(
            src_ref=fin_out.at[lax.rem(tok + step, 16)], dst_ref=fin_a.at[step], send_sem=pair_sem.at[4],
            recv_sem=pair_sem.at[5], device_id=tok_peer(step), device_id_type=MESH)

    def fin_b_copy(step):
        return pltpu.make_async_remote_copy(
            src_ref=fin_b.at[0], dst_ref=fin_b.at[step], send_sem=pair_sem.at[6],
            recv_sem=pair_sem.at[7], device_id=voc_peer(step), device_id_type=MESH)

    def start_all(copy):
        def body(step, carry):
            copy(step).start()
            return carry
        lax.fori_loop(1, 16, body, 0)

    def group(ref, first, at):
        view = ref.at[pl.ds(first, 15)]
        return pltpu.make_async_remote_copy(
            src_ref=view, dst_ref=view, send_sem=pair_sem.at[at], recv_sem=pair_sem.at[at + 1],
            device_id=tok_peer(1), device_id_type=MESH)

    sq_group, a2a_group, r_group = group(sq_buf, 1, 0), group(a2a_in, 0, 2), group(r_buf, 0, 8)
    fin_a_group, fin_b_group = group(fin_a, 1, 4), group(fin_b, 1, 6)

    start_all(a2a_copy)
    start_all(sq_copy)
    a2a_in[tok] = a2a_out[tok]

    gain_copy.start()
    ids_copy.start()
    student_copy.start()

    def load(index, carry):
        head_copy(index).start()
        return carry

    lax.fori_loop(0, 32, load, 0)

    place_of = []
    offset = jnp.int32(0)
    for pair in range(8):
        first, second = lens[2 * pair], lens[2 * pair + 1]
        low = jnp.where(lane < first, offset + lane, -1)
        high = jnp.where(lane - 64 < second, offset + first + lane - 64, -1)
        place_of.append(jnp.where(lane < 64, low, high))
        offset = offset + first + second
    place_of = jnp.concatenate(place_of, axis=1)

    def fill(block, carry):
        start = pl.multiple_of(block * 64, 64)
        want = lax.broadcasted_iota(jnp.int32, (64, 1024), 0) + start
        onehot[pl.ds(start, 64), :] = jnp.where(want == place_of, 1.0, 0.0).astype(BF16)
        return carry

    lax.fori_loop(0, cap // 64, fill, 0)


    gain_copy.wait()

    def spread_gain(row, carry):
        wide = jnp.broadcast_to(gain_in[pl.ds(row, 1), :], (128, 128)).T
        index = row // 2
        y = (index // 16) * 2 + index % 2
        start = pl.multiple_of((row % 2) * 4, 4)
        gcol[(index // 2) % 2, y, (index // 4) % 4, pl.ds(start, 4)] = wide.reshape(4, 32, 128)
        return carry

    lax.fori_loop(0, 32, spread_gain, 0, unroll=2)
    a2a_group.wait_recv()
    pieces = []
    for pair in range(8):
        low, high = a2a_in[2 * pair].astype(F32), a2a_in[2 * pair + 1].astype(F32)
        upper = jnp.where(lane < 64, low, pltpu.roll(high, 64, 1))
        under = jnp.where(lane < 64, pltpu.roll(low, 64, 1), high)
        pieces.append(jnp.concatenate([upper, under], axis=0))
    block = jnp.concatenate(pieces, axis=1).astype(BF16)
    packed = lax.dot_general(block, onehot[...], (((1,), (1,)), ((), ())), preferred_element_type=F32)

    numbers = {}

    def number_of(*key):
        return numbers.setdefault(key, len(numbers))

    def push(n, sent, key, src, target):
        if n == 2 and not has_z:
            return
        pltpu.make_async_remote_copy(
            src_ref=src, dst_ref=src, send_sem=send_sem.at[3 * n + sent], recv_sem=recv_sem.at[number_of(n, *key)],
            device_id=target, device_id_type=MESH).start()

    def arrive(n, key, view):
        if n == 2 and not has_z:
            return
        pltpu.make_async_remote_copy(
            src_ref=view, dst_ref=view, send_sem=send_sem.at[0], recv_sem=recv_sem.at[number_of(n, *key)],
            device_id=mate, device_id_type=MESH).wait_recv()

    mate = device(here, 1 - core)
    y, x, z = here["y"], here["x"], here["z"]
    own = [slab.at[core, y, x, z] for slab in slabs]
    for n in range(3):
        for at, (start, row, rows) in enumerate(blocks[n]):
            slabs[n][core, y, x, z, 32 * at:32 * at + rows] = packed[row:row + rows, start:start + 128].astype(BF16)
        if n < 2:
            for by in (4, 3, 5, 2, 6, 1, 7):
                push(n, 0, ("first",), own[n], device(moved("z", by), core))
        elif has_z:
            for step in (10, 2, 8, 6, 9, 11, 14, 1, 3, 4, 12, 5, 7, 13, 15):
                push(n, 0, ("first",), own[n], plane_peer(step))
    firsts = [slabs[0].at[core, y, x, pl.ds(0, 7)], slabs[1].at[core, y, x, pl.ds(0, 7)],
              slabs[2].at[core, pl.ds(0, 3), 0, pl.ds(0, 5)]]
    sent_views = []
    for n in (0, 1):
        sent_views += [firsts[n], slabs[n].at[0], slabs[n].at[:, :, pl.ds(0, 3), pl.ds(0, 5)]]
    if has_z:
        sent_views += [firsts[2], slabs[2].at[0, :, :, pl.ds(0, 7)], slabs[2].at[0]]

    sq_group.wait_recv()
    total_sq = sq_buf[0]
    for step in range(1, 16):
        total_sq = total_sq + sq_buf[step]
    r_buf[tok] = lax.rsqrt(total_sq / D + EPS)
    start_all(r_copy)

    lax.fori_loop(32, 64, spread_gain, 0, unroll=2)

    def zero(block, carry):
        acc[pl.ds(pl.multiple_of(block * 64, 64), 64), :] = jnp.zeros((64, 512), F32)
        return carry

    lax.fori_loop(0, cap // 64, zero, 0)

    def piece(n, which, c_at, b_at):
        if n == 0:
            return slabs[0].at[which, b_at, c_at]
        return slabs[1].at[which, c_at, b_at]

    def plane(n, which, c_at):
        if n == 0:
            return slabs[0].at[which, :, c_at]
        if n == 1:
            return slabs[1].at[which, c_at]
        return slabs[2].at[which, :, :, c_at]

    def zhalf(c_at, half):
        return slabs[2].at[core, pl.ds(2 * half, 2), :, c_at]

    second = ("y", "x")

    def two_lines(n):
        return slabs[0].at[core, pl.ds(0, 2), x] if n == 0 else slabs[1].at[core, y, pl.ds(0, 2)]

    def two_planes(n, which):
        if n == 0:
            return slabs[0].at[which, :, pl.ds(0, 2)]
        if n == 1:
            return slabs[1].at[which, pl.ds(0, 2)]
        return slabs[2].at[which, :, :, pl.ds(0, 2)]

    def both_ways(n, name, b_at):
        axis = lasts[n]
        for side in (1, -1):
            push(n, 1, (name,), piece(n, core, here[axis], b_at), device(moved(axis, side), core))

    def go_on(n, name, b_at):
        axis = lasts[n]
        arrive(n, (name,), two_lines(n))
        push(n, 2, (name, "on"), piece(n, core, moved(axis, -way)[axis], b_at), device(moved(axis, way), core))

    def multiply(n, which, pick):
        if n == 2 and not has_z:
            return
        for row, rows in ((0, 32), (0, 16), (16, 16)):
            chosen = [(at, block[0]) for at, block in enumerate(blocks[n]) if block[1:] == (row, rows)]
            if not chosen:
                continue
            take = (which, *pick, slice(row, row + rows))
            weight = gcol[take].reshape(-1, 128)
            depth = weight.shape[0]
            lefts = []
            for at, start in chosen:
                left = slabs[n][(which, *pick, slice(32 * at, 32 * at + rows))].astype(F32).reshape(depth, 128)
                lefts.append((left * r_rows[0:1, start:start + 128] * weight).astype(BF16))
            left = jnp.concatenate(lefts, axis=1) if len(lefts) > 1 else lefts[0]
            right = w_all[take].reshape(depth, 512)
            term = lax.dot_general(left, right, (((0,), (0,)), ((), ())), preferred_element_type=F32)
            first = chosen[0][1]
            acc[first:first + 128 * len(chosen), :] += term

    def shift(axis, by):
        return lax.rem(here[axis] + by, RING[axis])

    def each(count, work, wanted=True):
        if not wanted:
            return
        def body(index, carry):
            work(index)
            return carry
        lax.fori_loop(0, count, body, 0)

    def both_cores(index):
        return lax.rem(core + index, 2)

    def whole(n, which, by):
        at = shift(lasts[n], by)
        multiply(n, which, (VALL, at, VALL) if n == 0 else (at, VALL, VALL))

    def planes(which, count, first, stride=1):
        each(count, lambda index: multiply(2, which, (VALL, VALL, shift("z", first + stride * index))), has_z)

    def to_mate(n, sent, key, refs):
        for ref in refs:
            push(n, sent, ("mate", *key), ref, mate)

    def from_mate(n, key, view):
        arrive(n, ("mate", *key), view)

    for n in (0, 1):
        arrive(n, ("first",), firsts[n])
        axis = second[n]
        for side in (1, -1):
            push(n, 2, ("line",), piece(n, core, here[lasts[n]], here[axis]), device(moved(axis, side), core))
    for n in (0, 1):
        both_ways(n, "own", here[second[n]])
    arrive(2, ("first",), firsts[2])
    for half in (0, 1) if has_z else ():
        for side in (1, -1):
            push(2, 1, ("wave", 0, half), zhalf(z, half), device(moved("z", side), core))
    to_mate(2, 2, (0,), [plane(2, core, z)])

    r_group.wait_recv()
    factors = [jnp.where(lane < 64, r_buf[2 * pair], r_buf[2 * pair + 1]) for pair in range(8)]
    factors = jnp.concatenate(factors, axis=1)
    factors = jnp.broadcast_to(factors, (16, 1024))
    digit_row = lax.broadcasted_iota(jnp.int32, (16, 1024), 0)
    table = jnp.zeros((16, 1024), F32)
    for digit, value in enumerate(split3(factors)):
        table = jnp.where(digit_row == digit, value, table)
    table = lax.dot_general(table.astype(BF16), onehot[...], (((1,), (1,)), ((), ())), preferred_element_type=F32)
    r_rows[...] = jnp.broadcast_to(table[0:1] + table[1:2] + table[2:3], r_rows.shape)

    pltpu.make_async_copy(w_all, w_all, local_sem.at[4]).wait()

    def zstep(step):
        for half in (0, 1):
            arrive(2, ("wave", step, half), slabs[2].at[core, pl.ds(0, 2), :, pl.ds(0, 2)])
            for side in (1, -1):
                at = moved("z", -side * (step + 1))["z"]
                if step < 2:
                    push(2, 1, ("wave", step + 1, half), zhalf(at, half), device(moved("z", side), core))
            if step == 2:
                push(2, 1, ("wave", 3, half), zhalf(moved("z", -way * 3)["z"], half), device(moved("z", way), core))
        sides = (step + 1, -step - 1)
        to_mate(2, 2, (step + 1,), [plane(2, core, moved("z", by)["z"]) for by in sides])

    ids_copy.wait()
    local_id = ids_in[...] - (tok * 16 + voc) * 512
    local_id = jnp.where((local_id >= 0) & (local_id < 512), local_id, 512)
    digits = jnp.where(lax.broadcasted_iota(jnp.int32, (16, 1024), 0) == 0, local_id // 256, local_id % 256)
    digits = digits.astype(F32).astype(BF16)
    cols = lax.dot_general(onehot[...], digits, (((1,), (1,)), ((), ())), preferred_element_type=F32)
    id_cols[...] = cols[:, 0:1] * 256.0 + cols[:, 1:2]
    student_copy.wait()
    st_rows[...] = jnp.dot(onehot[...], st_all[...], preferred_element_type=F32).astype(BF16)

    for n in (0, 1):
        axis = second[n]
        arrive(n, ("line",), two_lines(n))
        push(n, 2, ("opposite",), piece(n, core, here[lasts[n]], moved(axis, -way)[axis]), device(moved(axis, way), core))
    for n in (0, 1):
        axis = second[n]
        both_ways(n, "left", moved(axis, -1)[axis])
        both_ways(n, "right", moved(axis, 1)[axis])
    zstep(0)
    planes(core, 3, 7)
    for n in (0, 1):
        go_on(n, "own", here[second[n]])
    for n in (0, 1):
        axis = second[n]
        arrive(n, ("opposite",), piece(n, core, here[lasts[n]], 0))
        both_ways(n, "far", moved(axis, 2)[axis])
    for n in (0, 1):
        to_mate(n, 2, (0,), [plane(n, core, here[lasts[n]])])
    from_mate(2, (0,), plane(2, 1 - core, z))
    from_mate(2, (1,), two_planes(2, 1 - core))
    planes(1 - core, 3, 7)
    zstep(1)

    def opposite(n, name, by):
        axis = second[n]
        b_at = moved(axis, by)[axis]
        arrive(n, (name, "on"), piece(n, core, here[lasts[n]], 0))
        c_at = moved(lasts[n], 2)[lasts[n]]
        to_mate(n, 2, ("far",) if name == "far" else ("early",), [piece(n, core, c_at, b_at)])

    for n in (0, 1):
        from_mate(n, (0,), plane(n, 1 - core, here[lasts[n]]))
        each(2, lambda index: whole(n, both_cores(index), 0))
    for n in (0, 1):
        go_on(n, "left", moved(second[n], -1)[second[n]])
    for n in (0, 1):
        go_on(n, "right", moved(second[n], 1)[second[n]])
    for n in (0, 1):
        opposite(n, "own", 0)
    planes(core, 2, 2, 4)
    zstep(2)
    from_mate(2, (2,), two_planes(2, 1 - core))
    planes(1 - core, 2, 2, 4)
    for n in (0, 1):
        go_on(n, "far", moved(second[n], 2)[second[n]])
    for n in (0, 1):
        to_mate(n, 1, (1,), [plane(n, core, moved(lasts[n], side)[lasts[n]]) for side in (1, -1)])
    each(2, lambda index: whole(0, core, 1 + 2 * index))
    planes(core, 2, 3, 2)
    for n in (0, 1):
        opposite(n, "left", -1)
    for n in (0, 1):
        opposite(n, "right", 1)
    each(2, lambda index: whole(1, core, 1 + 2 * index))
    for half in (0, 1):
        arrive(2, ("wave", 3, half), zhalf(z, 0))
    at = moved("z", 4)["z"]
    to_mate(2, 2, (4,), [plane(2, core, at)])
    from_mate(2, (3,), two_planes(2, 1 - core))
    planes(1 - core, 2, 3, 2)
    from_mate(0, (1,), two_planes(0, 1 - core))
    each(2, lambda index: whole(0, 1 - core, 1 + 2 * index))
    for n in (0, 1):
        opposite(n, "far", 2)
    from_mate(1, (1,), two_planes(1, 1 - core))
    each(2, lambda index: whole(1, 1 - core, 1 + 2 * index))
    from_mate(2, (4,), plane(2, 1 - core, at))
    each(2, lambda index: multiply(2, both_cores(index), (VALL, VALL, shift("z", 4))), has_z)
    for n in (0, 1):
        three = slabs[0].at[core, pl.ds(0, 3), x] if n == 0 else slabs[1].at[core, y, pl.ds(0, 3)]
        from_mate(n, ("early",), three)
        from_mate(n, ("far",), piece(n, 1 - core, here[lasts[n]], 0))
        each(2, lambda index: whole(n, both_cores(index), 2))

    lanes128 = lax.broadcasted_iota(jnp.int32, (64, 128), 1)
    lanes512 = lax.broadcasted_iota(jnp.int32, (64, 512), 1).astype(F32)

    def partials(start):
        take = pl.ds(start, 64)
        logits = acc[take, :]
        top = jnp.max(logits, axis=1, keepdims=True)
        low = logits - top
        expo = jnp.exp(low)
        total = jnp.sum(expo, axis=1, keepdims=True)
        cross = jnp.sum(expo * (low - st_rows[take, :].astype(F32)), axis=1, keepdims=True)
        pick = jnp.sum(jnp.where(lanes512 == id_cols[take, :], logits, 0.0), axis=1, keepdims=True)
        table = jnp.zeros((64, 128), F32)
        for at, value in enumerate((top, total, cross, pick)):
            for digit, part in enumerate(split3(value)):
                table = jnp.where(lanes128 == 8 * digit + at, part, table)
        stats[take, :] = table.astype(BF16)

    assert len(numbers) == (44 if has_z else 30)
    def partials256(block, carry):
        for piece in range(4):
            partials(pl.multiple_of(block * 256 + piece * 64, 64))
        return carry

    lax.fori_loop(0, cap // 256, partials256, 0)
    if cap % 256:
        partials(cap - 128)
        partials(cap - 64)
    spread = lax.dot_general(stats[...][:, 0:32], onehot[...], (((0,), (0,)), ((), ())), preferred_element_type=F32)
    spread = spread[0:8] + spread[8:16] + spread[16:24]
    for pair in range(8):
        rows4 = spread[:, 128 * pair:128 * (pair + 1)]
        turned4 = pltpu.roll(rows4, 64, 1)
        fin_out[2 * pair] = jnp.where(lane < 64, rows4[0:2], turned4[2:4])
        fin_out[2 * pair + 1] = jnp.where(lane < 64, turned4[0:2], rows4[2:4])
    start_all(fin_a_copy)
    fin_a[0] = fin_out[tok]
    for at, view in enumerate(sent_views):
        pltpu.make_async_remote_copy(
            src_ref=view, dst_ref=view, send_sem=send_sem.at[at], recv_sem=recv_sem.at[0], device_id=mate,
            device_id_type=MESH).wait_send()
    for copies in (sq_group, a2a_group, r_group):
        copies.wait_send()
    fin_a_group.wait_recv()

    def combine(ref):
        every = ref[...]
        top, total = every[:, 0:1, :], every[:, 1:2, :]
        cross, pick = pltpu.roll(top, 64, 2), pltpu.roll(total, 64, 2)
        most = jnp.max(top, axis=0, keepdims=True)
        gap = top - most
        scale = jnp.exp(gap)
        return (most[0], jnp.sum(scale * total, axis=0), jnp.sum(scale * (cross + gap * total), axis=0),
                jnp.sum(pick, axis=0))

    sub = lax.broadcasted_iota(jnp.int32, (8, 128), 0)

    def table_of(values):
        table = jnp.zeros((8, 128), F32)
        for at, value in enumerate(values):
            table = jnp.where(sub == at, value, table)
        return table

    top, total, cross, pick = combine(fin_a)
    fin_b[0] = jnp.concatenate(
        [jnp.where(lane < 64, top, pltpu.roll(cross, 64, 1)), jnp.where(lane < 64, total, pltpu.roll(pick, 64, 1))], axis=0)
    start_all(fin_b_copy)
    fin_b_group.wait_recv()
    top, total, cross, pick = combine(fin_b)
    log_total = jnp.log(total)
    kl = cross / total - log_total
    logprob = pick - (top + log_total)
    valid = lane < lens[tok]
    out[...] = table_of((jnp.where(valid, kl, 0.0), jnp.where(valid, logprob, 0.0)))
    fin_a_group.wait_send()
    fin_b_group.wait_send()


def run(groups, number, hidden, gain, lengths, ids, student, head):
    cap = (sum(groups) + 1) // 2 * 128
    hbm = pl.BlockSpec(memory_space=pl.ANY)
    return pl.pallas_call(
        functools.partial(kernel, groups),
        out_shape=jax.ShapeDtypeStruct((8, 128), F32),
        in_specs=[hbm, hbm, pl.BlockSpec(memory_space=pltpu.SMEM), hbm, hbm, hbm],
        out_specs=pl.BlockSpec(memory_space=pltpu.VMEM),
        scratch_shapes=[pltpu.VMEM((2, 4, 4, 8, 16 * max(count, 1), 128), BF16) for count in groups] + [
            pltpu.VMEM((2, 4, 4, 8, 32, 512), BF16),
            pltpu.VMEM((1024, 512), BF16),
            pltpu.VMEM((64, 512), BF16),
            pltpu.VMEM((64, 128), F32),
            pltpu.VMEM((1, 1024), jnp.int32),
            pltpu.VMEM((cap, 1024), BF16),
            pltpu.VMEM((cap, 512), BF16),
            pltpu.VMEM((cap, 1), F32),
            pltpu.VMEM((cap, 512), F32),
            pltpu.VMEM((cap, 128), BF16),
            pltpu.VMEM((2, 4, 4, 8, 32, 128), F32),
            pltpu.VMEM((8, cap), F32),
            pltpu.VMEM((16, 1, 128), F32),
            pltpu.VMEM((16, 1, 128), F32),
            pltpu.VMEM((16, 16, 128), BF16),
            pltpu.VMEM((16, 16, 128), BF16),
            pltpu.VMEM((16, 2, 128), F32),
            pltpu.VMEM((16, 2, 128), F32),
            pltpu.VMEM((16, 2, 128), F32),
            pltpu.SemaphoreType.DMA((5,)),
            pltpu.SemaphoreType.DMA((10,)),
            pltpu.SemaphoreType.DMA((9,)),
            pltpu.SemaphoreType.DMA((44 if groups[2] else 30,)),
        ],
        compiler_params=pltpu.CompilerParams(
            collective_id=number, has_side_effects=True, vmem_limit_bytes=60 * 1024 * 1024),
        name="gathered_head_%d" % (64 * sum(groups)),
    )(hidden, gain, lengths, ids, student, head)


SPLITS = ((3, 3, 2), (4, 4, 2), (6, 6, 4))


def per_device(hidden, gain, head_weight, student, token_ids, lengths):
    args = (hidden, gain.reshape(64, 128), lengths, token_ids.reshape(1, -1), student,
            head_weight.reshape(32, 8, 32, head_weight.shape[1]))
    if len(SPLITS) == 1:
        table = run(SPLITS[0], 0, *args)
    else:
        tokens = jnp.sum(lengths)
        which = sum((tokens > 64 * sum(groups)).astype(jnp.int32) for groups in SPLITS[:-1])
        table = lax.switch(which, [functools.partial(run, groups, at) for at, groups in enumerate(SPLITS)], *args)
    return table[0, :64], table[1, :64]


def solution(mesh):
    placed = (P("tok", "voc"), P(), P(None, ("tok", "voc")), P(None, ("tok", "voc")), P(), P())
    return jax.shard_map(
        per_device, mesh=mesh, in_specs=placed, out_specs=(P("tok"), P("tok")), check_vma=False
    )
```
